256 devices in a mesh: freq: 4 (over x), rx: 16 (over z, core), src: 4 (over y).
Axes of the slice: x: 4, y: 4, z: 8, core: 2. Of those that a mesh axis runs over, the one named last changes fastest.
Arguments:
- kernel: bfloat16 [2, 4, 8192, 8192], P(None, 'freq', 'rx', 'src'), may hold values from -5 to 5
- data: float32 [2, 4, 8192, 128], P(None, 'freq', 'rx'), may hold values from -100 to 100
Outputs:
- solution: float32 [2, 4, 8192, 128], P(None, 'freq', 'src')
- direction: float32 [2, 4, 8192, 128], P(None, 'freq', 'src')
The draws below stay inside these ranges and needn't reach their ends.
All inputs are finite; a program needn't handle non-finite values.
Results may differ from the reference program's by a relative error of at most 0.011.
Values may be sent and summed in bfloat16 or wider, within the bound.
A program may use at most 64 MiB of HBM per device.

```python
import math
import jax
import jax.numpy as jnp
from jax import lax

NR = 8192
NS = 8192
NV = 128
ITERS = 2
FREQS = 4


def freq_amplitude(key, spread):
    order_key, jitter_key = jax.random.split(key, 2)
    order = jax.random.permutation(order_key, FREQS).astype(jnp.float32)
    jitter = jax.random.uniform(jitter_key, (FREQS,), jnp.float32, 0.0, 1.0)
    log_amp = -spread + 2.0 * spread * (order + jitter) / FREQS
    return jnp.exp(log_amp).reshape(1, FREQS, 1, 1)


def lax_iota_rows():
    return jnp.arange(NR, dtype=jnp.int32)


def draw_kernel(key, part):
    key = jax.random.fold_in(key, 11)
    first = jax.random.fold_in(key, 0)
    second = jax.random.fold_in(key, 1)
    third = jax.random.fold_in(key, 2)
    fifth = jax.random.fold_in(key, 4)
    shape = (2, FREQS, NR, NS)
    noise = jnp.clip(jax.random.normal(first, shape, jnp.float32), -6.0, 6.0)
    offdiag = noise * (0.3 / jnp.sqrt(2.0 * NS))
    real_diag = jax.random.uniform(second, (1, FREQS, NR, 1), jnp.float32, 0.8, 1.2)
    imag_diag = jax.random.uniform(third, (1, FREQS, NR, 1), jnp.float32, -0.3, 0.3)
    diag = jnp.concatenate([real_diag, imag_diag], axis=0)
    rows = lax_iota_rows()
    eye = (rows[:, None] == jnp.arange(NS, dtype=jnp.int32)[None, :]).astype(jnp.float32)
    result = (offdiag + diag * eye) * freq_amplitude(fifth, 0.6)
    return result.astype(jnp.bfloat16)


def draw_data(key, part):
    key = jax.random.fold_in(key, 12)
    first = jax.random.fold_in(key, 0)
    fourth = jax.random.fold_in(key, 3)
    shape = (2, FREQS, NR, NV)
    rising = 0.5 + jnp.arange(NR, dtype=jnp.float32)[None, None, :, None] / NR
    amplitude = freq_amplitude(fourth, 1.2)
    noise = jnp.clip(jax.random.normal(first, shape, jnp.float32), -6.0, 6.0)
    return noise * rising * amplitude


def setup_inputs(seed: int = 0) -> dict:
    streams_of = jax.random.split(jax.random.key(seed), 3)
    return {
        "kernel": draw_kernel(jax.random.fold_in(streams_of[2], 71), 0),
        "data": draw_data(jax.random.fold_in(streams_of[2], 71), 0),
    }


def to_cat(field):
    return jnp.concatenate([field[0], field[1]], axis=-1)

def from_cat(field, width):
    return jnp.stack([field[..., :width], field[..., width:]])

def apply_forward(kernel, vector, width):
    rounded = vector.astype(jnp.bfloat16)
    results = []
    for freq_index in range(FREQS):
        first = jnp.dot(kernel[0, freq_index], rounded[freq_index], preferred_element_type=jnp.float32)
        second = jnp.dot(kernel[1, freq_index], rounded[freq_index], preferred_element_type=jnp.float32)
        results.append(jnp.concatenate([first[:, :width] - second[:, width:], first[:, width:] + second[:, :width]], axis=1))
    return jnp.stack(results)

def apply_adjoint(kernel, vector, width):
    rounded = vector.astype(jnp.bfloat16)
    dims = (((0,), (0,)), ((), ()))
    results = []
    for freq_index in range(FREQS):
        piece = rounded[freq_index]
        swapped = jnp.concatenate([piece[:, width:], -piece[:, :width]], axis=1)
        term = lax.dot_general(kernel[0, freq_index], piece, dims, preferred_element_type=jnp.float32)
        term = term + lax.dot_general(kernel[1, freq_index], swapped, dims, preferred_element_type=jnp.float32)
        results.append(term)
    return jnp.stack(results)

def vec_norm(field):
    return jnp.sqrt(jnp.sum(field * field))

def reference(kernel, data):
    width = data.shape[3]
    u_state = to_cat(data)
    beta = vec_norm(u_state)
    u_state = u_state / beta
    q_state = apply_adjoint(kernel, u_state, width)
    alpha = vec_norm(q_state)
    v_state = q_state / alpha
    w_state = v_state
    x_state = jnp.zeros_like(v_state)
    phibar = beta
    rhobar = alpha
    for step in range(ITERS):
        p_state = apply_forward(kernel, v_state, width) - alpha * u_state
        beta = vec_norm(p_state)
        u_state = p_state / beta
        q_state = apply_adjoint(kernel, u_state, width) - beta * v_state
        alpha = vec_norm(q_state)
        v_state = q_state / alpha
        rho = jnp.sqrt(rhobar * rhobar + beta * beta)
        cosine = rhobar / rho
        sine = beta / rho
        theta = sine * alpha
        rhobar = -cosine * alpha
        phi = cosine * phibar
        phibar = sine * phibar
        x_state = x_state + phi / rho * w_state
        w_state = v_state - theta / rho * w_state
    factor = math.sqrt(2.0 * FREQS * NS * NV)
    return (from_cat(x_state, width), from_cat(w_state * factor, width))
```

```python
import functools
import math

import jax
import jax.numpy as jnp
from jax import lax
from jax.experimental import pallas as pl
from jax.experimental.pallas import tpu as pltpu
from jax.sharding import PartitionSpec as P

GROUPS = 1
ITERS = 2
PH = ITERS + 1
CH = 256
MESH = pl.DeviceIdType.MESH
F32 = jnp.float32
BF16 = jnp.bfloat16
NN = (((1,), (0,)), ((), ()))
NT = (((1,), (1,)), ((), ()))


def tile_of_squares(x):
    sq = x * x
    rows, lanes = sq.shape
    part = jnp.sum(sq.reshape(rows // 8, 8, lanes), axis=0)
    total = part[:, :128]
    for i in range(1, lanes // 128):
        total = total + part[:, i * 128 : (i + 1) * 128]
    return total


def total_of(tile):
    return jnp.sum(tile, axis=(0, 1), keepdims=True)


def lsqr_kernel(dims, g_hbm, data_ref, q_out, coef_ref, g_v, d_t, p_st, lhs, own, q_prev, acc, sib_s, sib_r, rs_s, rs_r,
                ag, y_s, y_r, nsq, sq_b, sp1_b, sp2_b, g_sem, out_sem, sib_ss, sib_rs, rs_ss, rs_rs, ag_ss, ag_rs,
                as_ss, as_rs, y_ss, y_rs, sq_ss, sq_rs, sp1_ss, sp1_rs, sp2_ss, sp2_rs):
    nx, ny, nz, rows, cols, width = dims
    half = width // 2
    vr = half // GROUPS
    R = 2 * vr
    G = range(GROUPS)
    x = lax.axis_index("freq")
    y = lax.axis_index("src")
    rx = lax.axis_index("rx")
    me = rx // 2
    core = lax.rem(rx, 2)
    sib = {"rx": rx + 1 - 2 * core}

    def zp(off):
        return {"rx": lax.rem(rx + 2 * off + 2 * nz, 2 * nz)}

    def yp(off):
        return {"src": lax.rem(y + off, ny)}

    def chunk(off):
        return lax.rem(me + off + nz, nz)

    started = []

    def rc(src, dst, ss, rs, dev, keep=True):
        c = pltpu.make_async_remote_copy(src_ref=src, dst_ref=dst, send_sem=ss, recv_sem=rs, device_id=dev, device_id_type=MESH)
        c.start()
        if keep:
            started.append(c)

    def wait_recv(dst, ss, rs):
        pltpu.make_async_remote_copy(src_ref=dst, dst_ref=dst, send_sem=ss, recv_sem=rs, device_id=sib, device_id_type=MESH).wait_recv()

    def wait_send(src, ss, rs):
        pltpu.make_async_remote_copy(src_ref=src, dst_ref=src, send_sem=ss, recv_sem=rs, device_id=sib, device_id_type=MESH).wait_send()

    def far_off(t):
        e = lax.rem(t, 2)
        return nz // 2 + (1 - e) * (t // 2) - e * ((t + 1) // 2)

    def g_copy(t):
        ch = chunk(far_off(t))
        lanes = pl.ds(pl.multiple_of(ch * CH, CH), CH)
        return pltpu.make_async_copy(g_hbm.at[:, lanes], g_v.at[:, lanes], g_sem.at[t])

    barrier = pltpu.get_barrier_semaphore()
    peers = [zp(o) for o in range(1, nz)] + [sib]
    xy = [(dx, dy) for dx in range(nx) for dy in range(ny) if dx or dy]

    def xyp(dx, dy):
        return {"freq": lax.rem(x + dx, nx), "src": lax.rem(y + dy, ny)}

    def xcp(dx):
        return {"freq": lax.rem(x + dx, nx), "rx": rx + 1 - 2 * core}

    peers += [xyp(dx, dy) for dx, dy in xy]
    peers += [xcp(dx) for dx in range(1, nx)]
    for t in range(nz):
        g_copy(t).start()
    for p in peers:
        pl.semaphore_signal(barrier, inc=1, device_id=p, device_id_type=MESH)

    for c in range(2):
        d_t[c] = data_ref[c].T
    for g in G:
        for pos in range(2):
            h = core if pos == 0 else 1 - core
            base = pl.multiple_of(h * half + g * vr, vr)
            for c in range(2):
                p_st[g, pos, pl.ds(c * vr, vr), :] = d_t[c, pl.ds(base, vr), :]
    pl.semaphore_wait(barrier, len(peers))

    def sp1_send(k, tile):
        slot = 2 * x + core
        sp1_b[k, slot] = tile
        for i, dev in enumerate([sib] + [f(dx) for dx in range(1, nx) for f in (lambda d: xyp(d, 0), xcp)]):
            rc(sp1_b.at[k, slot], sp1_b.at[k, slot], sp1_ss.at[k, i], sp1_rs.at[k, slot], dev)

    def sp1_wait_sp2_send(k):
        for dx in range(nx):
            for dc in range(2):
                if dx or dc:
                    slot = 2 * lax.rem(x + dx, nx) + lax.rem(core + dc, 2)
                    wait_recv(sp1_b.at[k, slot], sp1_ss.at[k, 0], sp1_rs.at[k, slot])
        tile = sp1_b[k, 0]
        for i in range(1, 2 * nx):
            tile = tile + sp1_b[k, i]
        sp2_b[k, me] = tile
        for i in range(1, nz):
            rc(sp2_b.at[k, me], sp2_b.at[k, me], sp2_ss.at[k, i], sp2_rs.at[k, me], zp(i))

    def sp2_wait(k):
        for i in range(1, nz):
            slot = chunk(i)
            wait_recv(sp2_b.at[k, slot], sp2_ss.at[k, i], sp2_rs.at[k, slot])
        tile = sp2_b[k, 0]
        for i in range(1, nz):
            tile = tile + sp2_b[k, i]
        return jnp.sqrt(total_of(tile))

    def sq_send(k):
        total = None
        for g in G:
            for pos in range(2):
                part = nsq[g, pos, 0]
                for ch in range(1, nz):
                    part = part + nsq[g, pos, ch]
                both = part if pos == 0 else both + part
            total = both if g == 0 else total + both
        slot = x * ny + y
        sq_b[k, slot] = total
        for i, (dx, dy) in enumerate(xy):
            rc(sq_b.at[k, slot], sq_b.at[k, slot], sq_ss.at[k, i], sq_rs.at[k, slot], xyp(dx, dy))

    def sq_wait(k):
        for dx, dy in xy:
            slot = lax.rem(x + dx, nx) * ny + lax.rem(y + dy, ny)
            wait_recv(sq_b.at[k, slot], sq_ss.at[k, 0], sq_rs.at[k, slot])
        tile = sq_b[k, 0]
        for i in range(1, nx * ny):
            tile = tile + sq_b[k, i]
        return jnp.sqrt(total_of(tile))

    def p_norm_tile():
        total = None
        for g in G:
            for pos in range(2):
                t = tile_of_squares(p_st[g, pos])
                total = t if total is None else total + t
        return total

    def a1(k, g):
        for pos in range(2):
            u = p_st[g, pos]
            hi = u.astype(BF16)
            lo = (u - hi.astype(F32)).astype(BF16)
            for i, part in enumerate((hi, lo)):
                r0 = (2 * i + pos) * R
                lhs[g, pl.ds(r0, R), pl.ds(0, rows)] = part
                lhs[g, pl.ds(r0, vr), pl.ds(rows, rows)] = part[vr:]
                lhs[g, pl.ds(r0 + vr, vr), pl.ds(rows, rows)] = -part[:vr]

        def step(t, carry):
            ch = chunk(far_off(t))
            if k == 0 and g == 0:
                g_copy(t).wait()
            lanes = pl.ds(pl.multiple_of(ch * CH, CH), CH)
            res = lax.dot_general(lhs[g], g_v[:, lanes], NN, preferred_element_type=F32)
            both = res[: 2 * R] + res[2 * R :]
            own[g, ch] = both[:R]
            sib_s[k, g, ch] = both[R:]
            rc(sib_s.at[k, g, ch], sib_r.at[k, g, ch], sib_ss.at[k, g, t], sib_rs.at[k, g, t], sib, keep=False)
            return carry

        lax.fori_loop(0, nz, step, 0)

    def a2(k, g):
        def pair(t):
            ch = chunk(far_off(t))
            wait_recv(sib_r.at[k, g, ch], sib_ss.at[k, g, t], sib_rs.at[k, g, t])
            return ch, own[g, ch] + sib_r[k, g, ch]

        def step(t, carry):
            ch, s = pair(t)
            off = far_off(t)
            rs_s[k, g, off] = s.astype(BF16)
            rc(rs_s.at[k, g, off], rs_r.at[k, g, off], rs_ss.at[k, g, off], rs_rs.at[k, g, off], zp(off), keep=False)
            return carry

        lax.fori_loop(0, nz - 1, step, 0)
        ch, s = pair(nz - 1)
        return s

    def a3(k, g, s, inv_beta, coef):
        for off in (1, nz - 1, 2, nz - 2, 3, nz - 3, 4):
            wait_recv(rs_r.at[k, g, off], rs_ss.at[k, g, off], rs_rs.at[k, g, off])
            s = s + rs_r[k, g, off].astype(F32)
        q = s * inv_beta
        if k:
            q = q - coef * q_prev[g]
        q_prev[g] = q
        ag[k, g, 0, me] = q.astype(BF16)
        mine = ag.at[k, g, 0, me]
        for off in (2, nz - 2, 1, nz - 1):
            rel = (nz - off) % nz
            rc(mine, mine, ag_ss.at[k, g, off], ag_rs.at[k, g, rel], zp(off))
        rc(mine, ag.at[k, g, 1, me], as_ss.at[k, g, 0], as_rs.at[k, g, 0], sib)

    def a4(k, g):
        hr = R // 2

        def z_wait(off):
            ch = chunk(off)
            if off == 4:
                wait_recv(ag.at[k, g, 0, ch, pl.ds(0, hr)], ag_ss.at[k, g, 4], ag_rs.at[k, g, 4])
                wait_recv(ag.at[k, g, 0, ch, pl.ds(hr, hr)], ag_ss.at[k, g, 0], ag_rs.at[k, g, 0])
            else:
                wait_recv(ag.at[k, g, 0, ch], ag_ss.at[k, g, off], ag_rs.at[k, g, off])

        def to_sib(off):
            ch = chunk(off)
            rc(ag.at[k, g, 0, ch], ag.at[k, g, 1, ch], as_ss.at[k, g, off], as_rs.at[k, g, off], sib)

        z_wait(2)
        c2 = ag.at[k, g, 0, chunk(2)]
        rc(c2, c2, ag_ss.at[k, g, 3], ag_rs.at[k, g, 3], zp(nz - 1))
        h0 = ag.at[k, g, 0, chunk(2), pl.ds(0, hr)]
        rc(h0, h0, ag_ss.at[k, g, 4], ag_rs.at[k, g, 4], zp(nz - 2))
        z_wait(nz - 2)
        c6 = ag.at[k, g, 0, chunk(nz - 2)]
        rc(c6, c6, ag_ss.at[k, g, 5], ag_rs.at[k, g, 5], zp(1))
        h1 = ag.at[k, g, 0, chunk(nz - 2), pl.ds(hr, hr)]
        rc(h1, h1, ag_ss.at[k, g, 0], ag_rs.at[k, g, 0], zp(2))
        to_sib(2)
        to_sib(nz - 2)
        for off in (1, nz - 1, 3, nz - 3, 4):
            z_wait(off)
            to_sib(off)

    order = (0, 2, nz - 2, 1, nz - 1, 3, nz - 3, 4)

    def sib_wait(k, g, off):
        wait_recv(ag.at[k, g, 1, chunk(off)], as_ss.at[k, g, off], as_rs.at[k, g, off])

    def f1(k, g):
        for n, off in enumerate(order):
            ch = chunk(off)
            sib_wait(k, g, off)
            lanes = pl.ds(pl.multiple_of(ch * CH, CH), CH)
            v0 = ag[k, g, 0, ch]
            v1 = ag[k, g, 1, ch]
            v = jnp.concatenate([v0, v1], axis=0)
            w = jnp.concatenate([-v0[vr:], v0[:vr], -v1[vr:], v1[:vr]], axis=0)
            res = lax.dot_general(v, g_v[pl.ds(0, rows), lanes], NT, preferred_element_type=F32)
            res = res + lax.dot_general(w, g_v[pl.ds(rows, rows), lanes], NT, preferred_element_type=F32)
            if n == 0:
                acc[g] = res
            else:
                acc[g] += res
        y_s[k, g] = acc[g].astype(BF16)
        for off in (2, 1, 3):
            rc(y_s.at[k, g], y_r.at[k, g, off], y_ss.at[k, g, off], y_rs.at[k, g, off], yp(off))

    def q_norms(k, g):
        for pos in range(2):
            for ch in range(nz):
                nsq[g, pos, ch] = tile_of_squares(ag[k, g, pos, ch].astype(F32))

    def f2(k, g, inv_alpha, coef):
        for off in (1, 3, 2):
            wait_recv(y_r.at[k, g, off], y_ss.at[k, g, off], y_rs.at[k, g, off])
        for pos in range(2):
            sl = pl.ds(pos * R, R)
            s = acc[g, sl]
            for off in (1, 2, 3):
                s = s + y_r[k, g, off, sl].astype(F32)
            p_st[g, pos] = s * inv_alpha - coef * p_st[g, pos]

    def out_copy(k):
        return pltpu.make_async_copy(ag.at[k], q_out.at[k], out_sem.at[k])

    alphas, betas = [], []
    for k in range(PH):
        sp1_send(k, p_norm_tile())
        for g in G:
            a1(k, g)
        sp1_wait_sp2_send(k)
        sums = [a2(k, g) for g in G]
        beta = sp2_wait(k)
        betas.append(beta)
        inv_beta = 1.0 / beta
        for g in G:
            a3(k, g, sums[g], inv_beta, beta / alphas[-1] if k else None)
        for g in G:
            a4(k, g)
        if k < ITERS:
            for g in G:
                f1(k, g)
            for g in G:
                q_norms(k, g)
            sq_send(k)
            out_copy(k).start()
            alpha = sq_wait(k)
            alphas.append(alpha)
            for g in G:
                f2(k, g, 1.0 / alpha, alpha / beta)
        else:
            for g in G:
                for off in order:
                    sib_wait(k, g, off)
                q_norms(k, g)
            sq_send(k)
            out_copy(k).start()
            alphas.append(sq_wait(k))

    factor = math.sqrt(2.0 * nx * cols * ny * width)
    phibar, rhobar = betas[0], alphas[0]
    x_w = [None] * PH
    w_w = [1.0 / alphas[0]] + [None] * ITERS
    for it in range(ITERS):
        beta, alpha = betas[it + 1], alphas[it + 1]
        rho = jnp.sqrt(rhobar * rhobar + beta * beta)
        cosine, sine = rhobar / rho, beta / rho
        theta = sine * alpha
        rhobar = -cosine * alpha
        phi = cosine * phibar
        phibar = sine * phibar
        step, back = phi / rho, theta / rho
        for j in range(it + 1):
            x_w[j] = step * w_w[j] if x_w[j] is None else x_w[j] + step * w_w[j]
            w_w[j] = -back * w_w[j]
        w_w[it + 1] = 1.0 / alpha
    for j in range(ITERS):
        coef_ref[j] = jnp.broadcast_to(x_w[j], (8, 128))
    for j in range(PH):
        coef_ref[ITERS + j] = jnp.broadcast_to(w_w[j] * factor, (8, 128))

    for k in range(PH):
        out_copy(k).wait()
    for c in started:
        c.wait_send()
    for k in range(PH):
        for g in G:
            def fin(t, carry, k=k, g=g):
                wait_send(sib_s.at[k, g, t], sib_ss.at[k, g, t], sib_rs.at[k, g, t])
                return carry
            lax.fori_loop(0, nz, fin, 0)

            def fin2(t, carry, k=k, g=g):
                wait_send(rs_s.at[k, g, t], rs_ss.at[k, g, t], rs_rs.at[k, g, t])
                return carry
            lax.fori_loop(1, nz, fin2, 0)


def finish_kernel(dims, q_ref, coef_ref, x_ref, w_ref, buf):
    nx, ny, nz, rows, cols, width = dims
    half = width // 2
    vr = half // GROUPS
    core = lax.rem(lax.axis_index("rx"), 2)
    cf = [coef_ref[j, 0:1, 0:1] for j in range(ITERS + PH)]
    for g in range(GROUPS):
        for pos in range(2):
            h = core if pos == 0 else 1 - core
            base = pl.multiple_of(h * half + g * vr, vr)
            q = [q_ref[k, g, pos, 0].astype(F32) for k in range(PH)]
            xv = cf[0] * q[0]
            for j in range(1, ITERS):
                xv = xv + cf[j] * q[j]
            wv = cf[ITERS] * q[0]
            for j in range(1, PH):
                wv = wv + cf[ITERS + j] * q[j]
            for c in range(2):
                buf[0, c, pl.ds(base, vr), :] = xv[c * vr : (c + 1) * vr]
                buf[1, c, pl.ds(base, vr), :] = wv[c * vr : (c + 1) * vr]
    for c in range(2):
        x_ref[c, 0] = buf[0, c].T
        w_ref[c, 0] = buf[1, c].T


def on_device(nx, ny, nz, kernel, data):
    rows, cols, width = kernel.shape[2], kernel.shape[3], data.shape[3]
    dims = (nx, ny, nz, rows, cols, width)
    R = width // GROUPS
    G = GROUPS
    sem = pltpu.SemaphoreType.DMA
    vm = pltpu.VMEM
    q_all, coefs = pl.pallas_call(
        functools.partial(lsqr_kernel, dims),
        name="lsqr",
        out_shape=(
            jax.ShapeDtypeStruct((PH, G, 2, nz, R, CH), BF16),
            jax.ShapeDtypeStruct((ITERS + PH, 8, 128), F32),
        ),
        in_specs=[pl.BlockSpec(memory_space=pl.ANY), pl.BlockSpec(memory_space=pltpu.VMEM)],
        out_specs=(pl.BlockSpec(memory_space=pl.ANY), pl.BlockSpec(memory_space=pltpu.VMEM)),
        scratch_shapes=[
            vm((2 * rows, cols), BF16),
            vm((2, width, rows), F32),
            vm((G, 2, R, rows), F32),
            vm((G, 4 * R, 2 * rows), BF16),
            vm((G, nz, R, CH), F32),
            vm((G, R, CH), F32),
            vm((G, 2 * R, rows), F32),
            vm((PH, G, nz, R, CH), F32),
            vm((PH, G, nz, R, CH), F32),
            vm((PH, G, nz, R, CH), BF16),
            vm((PH, G, nz, R, CH), BF16),
            vm((PH, G, 2, nz, R, CH), BF16),
            vm((ITERS, G, 2 * R, rows), BF16),
            vm((ITERS, G, ny, 2 * R, rows), BF16),
            vm((G, 2, nz, 8, 128), F32),
            vm((PH, nx * ny, 8, 128), F32),
            vm((PH, 2 * nx, 8, 128), F32),
            vm((PH, nz, 8, 128), F32),
            sem((nz,)),
            sem((PH,)),
            sem((PH, G, nz)), sem((PH, G, nz)),
            sem((PH, G, nz)), sem((PH, G, nz)),
            sem((PH, G, nz)), sem((PH, G, nz)),
            sem((PH, G, nz)), sem((PH, G, nz)),
            sem((ITERS, G, ny)), sem((ITERS, G, ny)),
            sem((PH, nx * ny)), sem((PH, nx * ny)),
            sem((PH, 2 * nx)), sem((PH, 2 * nx)),
            sem((PH, nz)), sem((PH, nz)),
        ],
        compiler_params=pltpu.CompilerParams(collective_id=0, has_side_effects=True, vmem_limit_bytes=56 << 20),
    )(kernel.reshape(2 * rows, cols), data[:, 0])
    out = jax.ShapeDtypeStruct((2, 1, cols, width), F32)
    return pl.pallas_call(
        functools.partial(finish_kernel, dims),
        name="finish",
        grid=(nz,),
        out_shape=(out, out),
        in_specs=[
            pl.BlockSpec((PH, G, 2, 1, R, CH), lambda i: (0, 0, 0, i, 0, 0)),
            pl.BlockSpec((ITERS + PH, 8, 128), lambda i: (0, 0, 0)),
        ],
        out_specs=(
            pl.BlockSpec((2, 1, CH, width), lambda i: (0, 0, i, 0)),
            pl.BlockSpec((2, 1, CH, width), lambda i: (0, 0, i, 0)),
        ),
        scratch_shapes=[vm((2, 2, width, CH), F32)],
    )(q_all, coefs)


def solution(mesh):
    nx, ny, nz = mesh.shape["freq"], mesh.shape["src"], mesh.shape["rx"] // 2
    return jax.shard_map(
        functools.partial(on_device, nx, ny, nz),
        mesh=mesh,
        in_specs=(P(None, "freq", "rx", "src"), P(None, "freq", "rx", None)),
        out_specs=(P(None, "freq", "src", None), P(None, "freq", "src", None)),
        check_vma=False,
    )
```

```python
import functools
import math

import jax
import jax.numpy as jnp
from jax import lax
from jax.experimental import pallas as pl
from jax.experimental.pallas import tpu as pltpu
from jax.sharding import PartitionSpec as P

GROUPS = 1
ITERS = 2
PH = ITERS + 1
CH = 256
MESH = pl.DeviceIdType.MESH
F32 = jnp.float32
BF16 = jnp.bfloat16
NN = (((1,), (0,)), ((), ()))
NT = (((1,), (1,)), ((), ()))


def tile_of_squares(x):
    sq = x * x
    rows, lanes = sq.shape
    part = jnp.sum(sq.reshape(rows // 8, 8, lanes), axis=0)
    total = part[:, :128]
    for i in range(1, lanes // 128):
        total = total + part[:, i * 128 : (i + 1) * 128]
    return total


def total_of(tile):
    return jnp.sum(tile, axis=(0, 1), keepdims=True)


FAR = (4, 3, 5, 2, 6, 1, 7, 0)
BATCHES = ((0, 2), (2, 3), (3, 5), (5, 8))
HILO = (True, True, False)


def lsqr_kernel(dims, g_hbm, data_hbm, q_out, coef_ref, g_v, data_ref, d_t, p_st, lhs, own, q_prev, acc, sib_s, sib_r, rs_s, rs_r,
                ag, y_s, y_r, nsq, sq_b, sp1_b, sp2_b, zc_b, g_sem, out_sem, sib_ss, sib_rs, rs_ss, rs_rs, ag_ss, ag_rs,
                as_ss, as_rs, y_ss, y_rs, sq_ss, sq_rs, sp1_ss, sp1_rs, sp2_ss, sp2_rs, zc_ss, zc_rs):
    nx, ny, nz, rows, cols, width = dims
    half = width // 2
    vr = half // GROUPS
    R = 2 * vr
    hr = R // 2
    G = range(GROUPS)
    x = lax.axis_index("freq")
    y = lax.axis_index("src")
    rx = lax.axis_index("rx")
    me = rx // 2
    core = lax.rem(rx, 2)
    sib = {"rx": rx + 1 - 2 * core}
    zps = [{"rx": lax.rem(rx + 2 * o, 2 * nz)} for o in range(nz)]
    zcs = [{"rx": lax.rem(rx + 2 * o, 2 * nz) + 1 - 2 * core} for o in range(nz)]
    ynb = [{"src": y + 1 - 2 * lax.rem(y, 2)}, {"src": ny - 1 - y}]
    xps = [{"freq": lax.rem(x + o, nx)} for o in range(nx)]
    xcs = [{"freq": lax.rem(x + o, nx), "rx": rx + 1 - 2 * core} for o in range(nx)]
    xy = [(dx, dy) for dx in range(nx) for dy in range(ny) if dx or dy]
    xys = [{"freq": lax.rem(x + dx, nx), "src": lax.rem(y + dy, ny)} for dx, dy in xy]
    chunks = [lax.rem(me + o, nz) for o in range(nz)]
    lanes = [pl.ds(pl.multiple_of(c * CH, CH), CH) for c in chunks]

    started = []

    def rc(src, dst, ss, rs, dev):
        c = pltpu.make_async_remote_copy(src_ref=src, dst_ref=dst, send_sem=ss, recv_sem=rs, device_id=dev, device_id_type=MESH)
        c.start()
        started.append(c)

    def drain():
        for c in started:
            c.wait_send()
        started.clear()

    def wait_recv(dst, ss, rs):
        pltpu.make_async_remote_copy(src_ref=dst, dst_ref=dst, send_sem=ss, recv_sem=rs, device_id=sib, device_id_type=MESH).wait_recv()

    def g_copy(t):
        sl = lanes[FAR[t]]
        return pltpu.make_async_copy(g_hbm.at[:, sl], g_v.at[:, sl], g_sem.at[t])

    barrier = pltpu.get_barrier_semaphore()
    peers = zps[1:] + zcs + xys + xcs[1:]
    data_copy = pltpu.make_async_copy(data_hbm, data_ref, g_sem.at[nz])
    data_copy.start()
    for t in range(nz):
        g_copy(t).start()
    for p in peers:
        pl.semaphore_signal(barrier, inc=1, device_id=p, device_id_type=MESH)

    def tiles_send(buf, slot, tile, ss, rs, devs):
        buf[slot] = tile
        for i, dev in enumerate(devs):
            rc(buf.at[slot], buf.at[slot], ss.at[i], rs.at[slot], dev)

    def tiles_wait(buf, n, slots, ss, rs):
        for slot in slots:
            wait_recv(buf.at[slot], ss.at[0], rs.at[slot])
        tile = buf[0]
        for i in range(1, n):
            tile = tile + buf[i]
        return tile

    def sp1_send(k):
        tile = None
        for g in G:
            for pos in range(2):
                t = tile_of_squares(p_st[g, pos])
                tile = t if tile is None else tile + t
        tiles_send(sp1_b.at[k], 2 * x + core, tile, sp1_ss.at[k], sp1_rs.at[k], [sib] + xps[1:] + xcs[1:])

    def sp1_wait_sp2_send(k):
        slots = [2 * lax.rem(x + dx, nx) + lax.rem(core + dc, 2) for dx in range(nx) for dc in range(2) if dx or dc]
        tile = tiles_wait(sp1_b.at[k], 2 * nx, slots, sp1_ss.at[k], sp1_rs.at[k])
        tiles_send(sp2_b.at[k], me, tile, sp2_ss.at[k], sp2_rs.at[k], zps[1:])

    def sp2_wait(k):
        return jnp.sqrt(total_of(tiles_wait(sp2_b.at[k], nz, chunks[1:], sp2_ss.at[k], sp2_rs.at[k])))

    def sq_send(k):
        total = None
        for g in G:
            for pos in range(2):
                part = nsq[g, pos, 0]
                for ch in range(1, nz):
                    part = part + nsq[g, pos, ch]
                both = part if pos == 0 else both + part
            total = both if g == 0 else total + both
        tiles_send(sq_b.at[k], x * ny + y, total, sq_ss.at[k], sq_rs.at[k], xys)

    def sq_tile(k):
        slots = [lax.rem(x + dx, nx) * ny + lax.rem(y + dy, ny) for dx, dy in xy]
        return tiles_wait(sq_b.at[k], nx * ny, slots, sq_ss.at[k], sq_rs.at[k])

    def last_norm_send(k):
        total = None
        for g in G:
            t = tile_of_squares(ag[k, g, 0, 0].astype(F32))
            total = t if total is None else total + t
        tiles_send(sq_b.at[k], x * ny + y, total, sq_ss.at[k], sq_rs.at[k], xys)

    def last_norm_mid(k):
        tiles_send(zc_b, rx, sq_tile(k), zc_ss, zc_rs, zcs + zps[1:])

    def last_norm_wait():
        slots = [lax.rem(rx + d, 2 * nz) for d in range(1, 2 * nz)]
        return jnp.sqrt(total_of(tiles_wait(zc_b, 2 * nz, slots, zc_ss, zc_rs)))

    def build(k, g):
        for pos in range(2):
            u = p_st[g, pos]
            hi = u.astype(BF16)
            parts = (hi, (u - hi.astype(F32)).astype(BF16)) if HILO[k] else (hi,)
            for i, part in enumerate(parts):
                r0 = (2 * i + pos) * R
                lhs[g, r0 : r0 + R, :rows] = part
                lhs[g, r0 : r0 + vr, rows:] = part[vr:]
                lhs[g, r0 + vr : r0 + R, rows:] = -part[:vr]

    def a1(k, g, batch):
        for t in range(*BATCHES[batch]):
            if k == 0 and g == 0:
                g_copy(t).wait()
            if HILO[k]:
                res = lax.dot_general(lhs[g], g_v[:, lanes[FAR[t]]], NN, preferred_element_type=F32)
                both = res[: 2 * R] + res[2 * R :]
            else:
                both = lax.dot_general(lhs[g, : 2 * R], g_v[:, lanes[FAR[t]]], NN, preferred_element_type=F32)
            own[g, t] = both[:R]
            sib_s[k, g, t] = both[R:]
        t0, t1 = BATCHES[batch]
        part = pl.ds(t0, t1 - t0)
        rc(sib_s.at[k, g, part], sib_r.at[k, g, part], sib_ss.at[k, g, batch], sib_rs.at[k, g, batch], sib)

    def rs_send(k, g, slot, to, lo=0, n=R):
        part = pl.ds(lo, n)
        rc(rs_s.at[k, g, slot, part], rs_r.at[k, g, slot, part], rs_ss.at[k, g, slot], rs_rs.at[k, g, slot], zps[to])

    def rs_wait(k, g, slot, lo=0, n=R):
        part = pl.ds(lo, n)
        wait_recv(rs_r.at[k, g, slot, part], rs_ss.at[k, g, slot], rs_rs.at[k, g, slot])

    def a2(k, g, batch):
        t0, t1 = BATCHES[batch]
        part = pl.ds(t0, t1 - t0)
        wait_recv(sib_r.at[k, g, part], sib_ss.at[k, g, batch], sib_rs.at[k, g, batch])
        for t in range(t0, t1):
            off = FAR[t]
            pair = own[g, t] + sib_r[k, g, t]
            if off == 4:
                rs_s[k, g, 4, :hr] = pair[:hr].astype(BF16)
                rs_s[k, g, 0, hr:] = pair[hr:].astype(BF16)
                rs_send(k, g, 4, 2, 0, hr)
                rs_send(k, g, 0, nz - 2, hr, hr)
            elif off in (0, 2, nz - 2):
                own[g, t] = pair
            else:
                rs_s[k, g, off] = pair.astype(BF16)
                rs_send(k, g, off, 1 if off in (1, 3) else nz - 1)

    def a2b(k, g):
        rs_wait(k, g, 3)
        rs_wait(k, g, 4, 0, hr)
        s = own[g, FAR.index(2)] + rs_r[k, g, 3].astype(F32)
        rs_s[k, g, 2, :hr] = (s[:hr] + rs_r[k, g, 4, :hr].astype(F32)).astype(BF16)
        rs_s[k, g, 2, hr:] = s[hr:].astype(BF16)
        rs_send(k, g, 2, 2)
        rs_wait(k, g, nz - 3)
        rs_wait(k, g, 0, hr, hr)
        s = own[g, FAR.index(nz - 2)] + rs_r[k, g, nz - 3].astype(F32)
        rs_s[k, g, nz - 2, :hr] = s[:hr].astype(BF16)
        rs_s[k, g, nz - 2, hr:] = (s[hr:] + rs_r[k, g, 0, hr:].astype(F32)).astype(BF16)
        rs_send(k, g, nz - 2, nz - 2)

    def ag_send(k, g, rel, to, lo=0, n=R, sem=None):
        there = (rel - to) % nz
        sem = there if sem is None else sem
        rc(ag.at[k, g, 0, rel, pl.ds(lo, n)], ag.at[k, g, 0, there, pl.ds(lo, n)], ag_ss.at[k, g, sem], ag_rs.at[k, g, sem], zps[to])

    def z_wait(k, g, rel):
        if rel == 4:
            wait_recv(ag.at[k, g, 0, 4, pl.ds(0, hr)], ag_ss.at[k, g, 4], ag_rs.at[k, g, 4])
            wait_recv(ag.at[k, g, 0, 4, pl.ds(hr, hr)], ag_ss.at[k, g, 0], ag_rs.at[k, g, 0])
        else:
            wait_recv(ag.at[k, g, 0, rel], ag_ss.at[k, g, rel], ag_rs.at[k, g, rel])

    def to_sib(k, g, rel, n=1):
        part = pl.ds(rel, n)
        rc(ag.at[k, g, 0, part], ag.at[k, g, 1, part], as_ss.at[k, g, rel], as_rs.at[k, g, rel], sib)

    def sib_wait(k, g, rel, n=1):
        part = pl.ds(rel, n)
        wait_recv(ag.at[k, g, 1, part], as_ss.at[k, g, rel], as_rs.at[k, g, rel])

    def a3(k, g, inv_beta, coef):
        s = own[g, FAR.index(0)]
        for off in (1, nz - 1, 2, nz - 2):
            rs_wait(k, g, off)
            s = s + rs_r[k, g, off].astype(F32)
        q = s * inv_beta
        if k:
            q = q - coef * q_prev[g]
        q_prev[g] = q
        ag[k, g, 0, 0] = q.astype(BF16)
        for to in (2, nz - 2, 1, nz - 1):
            ag_send(k, g, 0, to)
        to_sib(k, g, 0)

    def a4a(k, g):
        z_wait(k, g, 2)
        ag_send(k, g, 2, nz - 1)
        ag_send(k, g, 2, nz - 2, 0, hr, 4)
        z_wait(k, g, nz - 2)
        ag_send(k, g, nz - 2, 1)
        ag_send(k, g, nz - 2, 2, hr, hr, 0)
        z_wait(k, g, 1)
        to_sib(k, g, 1, 2)
        z_wait(k, g, nz - 1)
        to_sib(k, g, nz - 2, 2)

    def a4b(k, g):
        for rel in (3, nz - 3, 4):
            z_wait(k, g, rel)
            to_sib(k, g, rel)

    def f1(k, g, rel):
        v0 = ag[k, g, 0, rel]
        v1 = ag[k, g, 1, rel]
        v = jnp.concatenate([v0, v1], axis=0)
        w = jnp.concatenate([-v0[vr:], v0[:vr], -v1[vr:], v1[:vr]], axis=0)
        res = lax.dot_general(v, g_v[:rows, lanes[rel]], NT, preferred_element_type=F32)
        res = res + lax.dot_general(w, g_v[rows:, lanes[rel]], NT, preferred_element_type=F32)
        if rel == 0:
            acc[g] = res
        else:
            acc[g] += res

    def q_norms(k, g, rel):
        for pos in range(2):
            nsq[g, pos, chunks[rel]] = tile_of_squares(ag[k, g, pos, rel].astype(F32))

    YP = [(pos, slice(pos * R + n * hr, pos * R + n * hr + hr), 2 * n + pos) for n in range(2) for pos in range(2)]

    def y_send(k, g, step):
        for pos, sl, i in YP:
            if step:
                wait_recv(y_r.at[k, g, 0, sl], y_ss.at[k, g, 0, i], y_rs.at[k, g, 0, i])
                acc[g, sl] = acc[g, sl] + y_r[k, g, 0, sl].astype(F32)
            y_s[k, g, step, sl] = acc[g, sl].astype(BF16)
            dev = ynb[(pos + step) % 2]
            rc(y_s.at[k, g, step, sl], y_r.at[k, g, step, sl], y_ss.at[k, g, step, i], y_rs.at[k, g, step, i], dev)

    def f2(k, g, inv_alpha, coef):
        for pos, sl, i in YP:
            wait_recv(y_r.at[k, g, 1, sl], y_ss.at[k, g, 1, i], y_rs.at[k, g, 1, i])
            total = acc[g, sl] + y_r[k, g, 1, sl].astype(F32)
            rs = slice(sl.start - pos * R, sl.stop - pos * R)
            p_st[g, pos, rs] = total * inv_alpha - coef * p_st[g, pos, rs]

    def out_copy(k):
        return pltpu.make_async_copy(ag.at[k], q_out.at[k], out_sem.at[k])

    data_copy.wait()
    for c in range(2):
        d_t[c] = data_ref[c].T
    for g in G:
        for pos in range(2):
            h = core if pos == 0 else 1 - core
            base = pl.multiple_of(h * half + g * vr, vr)
            for c in range(2):
                p_st[g, pos, c * vr : (c + 1) * vr, :] = d_t[c, pl.ds(base, vr), :]
    build(0, 0)
    pl.semaphore_wait(barrier, len(peers))

    alphas, betas = [], []
    for k in range(PH):
        last = k == ITERS
        for g in G:
            if k:
                f2(k - 1, g, inv_alpha, alphas[-1] / betas[-1])
            if k or g:
                build(k, g)
            a1(k, g, 0)
            a1(k, g, 1)
            if g == GROUPS - 1:
                sp1_send(k)
            a2(k, g, 0)
            a2(k, g, 1)
            a1(k, g, 2)
        for g in G:
            a1(k, g, 3)
            a2(k, g, 2)
            a2(k, g, 3)
        sp1_wait_sp2_send(k)
        for g in G:
            a2b(k, g)
        betas.append(sp2_wait(k))
        inv_beta = 1.0 / betas[-1]
        coef = betas[-1] / alphas[-1] if k else None
        for g in G:
            a3(k, g, inv_beta, coef)
        if last:
            last_norm_send(k)
            for g in G:
                a4a(k, g)
            last_norm_mid(k)
            for g in G:
                a4b(k, g)
            drain()
            for g in G:
                for rel, n in ((0, 1), (1, 2), (nz - 2, 2), (3, 1), (nz - 3, 1), (4, 1)):
                    sib_wait(k, g, rel, n)
            out_copy(k).start()
            alphas.append(last_norm_wait())
            break
        for g in G:
            sib_wait(k, g, 0)
            f1(k, g, 0)
        for g in G:
            a4a(k, g)
        for g in G:
            sib_wait(k, g, 1, 2)
            f1(k, g, 1)
            f1(k, g, 2)
            sib_wait(k, g, nz - 2, 2)
            f1(k, g, nz - 2)
            f1(k, g, nz - 1)
        for g in G:
            for rel in (0, 1, 2, nz - 2, nz - 1):
                q_norms(k, g, rel)
        for g in G:
            a4b(k, g)
        for g in G:
            for rel in (3, nz - 3, 4):
                sib_wait(k, g, rel)
                f1(k, g, rel)
            y_send(k, g, 0)
        for g in G:
            for rel in (3, nz - 3, 4):
                q_norms(k, g, rel)
        sq_send(k)
        out_copy(k).start()
        for g in G:
            y_send(k, g, 1)
        drain()
        alphas.append(jnp.sqrt(total_of(sq_tile(k))))
        inv_alpha = 1.0 / alphas[-1]

    factor = math.sqrt(2.0 * nx * cols * ny * width)
    phibar, rhobar = betas[0], alphas[0]
    x_w = [None] * PH
    w_w = [1.0 / alphas[0]] + [None] * ITERS
    for it in range(ITERS):
        beta, alpha = betas[it + 1], alphas[it + 1]
        rho = jnp.sqrt(rhobar * rhobar + beta * beta)
        cosine, sine = rhobar / rho, beta / rho
        theta = sine * alpha
        rhobar = -cosine * alpha
        phi = cosine * phibar
        phibar = sine * phibar
        step, back = phi / rho, theta / rho
        for j in range(it + 1):
            x_w[j] = step * w_w[j] if x_w[j] is None else x_w[j] + step * w_w[j]
            w_w[j] = -back * w_w[j]
        w_w[it + 1] = 1.0 / alpha
    for j in range(ITERS):
        coef_ref[j] = jnp.broadcast_to(x_w[j], (8, 128))
    for j in range(PH):
        coef_ref[ITERS + j] = jnp.broadcast_to(w_w[j] * factor, (8, 128))

    for k in range(PH):
        out_copy(k).wait()


FIN = 4


def finish_kernel(dims, *refs):
    nx, ny, nz, rows, cols, width = dims
    q_refs, (coef_ref, x_ref, w_ref, buf) = refs[:FIN], refs[FIN:]
    half = width // 2
    vr = half // GROUPS
    core = lax.rem(lax.axis_index("rx"), 2)
    cf = [coef_ref[j, 0:1, 0:1] for j in range(ITERS + PH)]
    for n, q_ref in enumerate(q_refs):
        for g in range(GROUPS):
            for pos in range(2):
                h = core if pos == 0 else 1 - core
                base = pl.multiple_of(h * half + g * vr, vr)
                q = [q_ref[k, g, pos, 0].astype(F32) for k in range(PH)]
                xv = cf[0] * q[0]
                for j in range(1, ITERS):
                    xv = xv + cf[j] * q[j]
                wv = cf[ITERS] * q[0]
                for j in range(1, PH):
                    wv = wv + cf[ITERS + j] * q[j]
                for c in range(2):
                    buf[n, 0, c, pl.ds(base, vr), :] = xv[c * vr : (c + 1) * vr]
                    buf[n, 1, c, pl.ds(base, vr), :] = wv[c * vr : (c + 1) * vr]
        for c in range(2):
            x_ref[c, 0, n * CH : (n + 1) * CH] = buf[n, 0, c].T
            w_ref[c, 0, n * CH : (n + 1) * CH] = buf[n, 1, c].T


def on_device(nx, ny, nz, kernel, data):
    rows, cols, width = kernel.shape[2], kernel.shape[3], data.shape[3]
    dims = (nx, ny, nz, rows, cols, width)
    R = width // GROUPS
    G = GROUPS
    sem = pltpu.SemaphoreType.DMA
    vm = pltpu.VMEM
    q_all, coefs = pl.pallas_call(
        functools.partial(lsqr_kernel, dims),
        name="lsqr",
        out_shape=(
            jax.ShapeDtypeStruct((PH, G, 2, nz, R, CH), BF16),
            jax.ShapeDtypeStruct((ITERS + PH, 8, 128), F32),
        ),
        in_specs=[pl.BlockSpec(memory_space=pl.ANY), pl.BlockSpec(memory_space=pl.ANY)],
        out_specs=(pl.BlockSpec(memory_space=pl.ANY), pl.BlockSpec(memory_space=pltpu.VMEM)),
        scratch_shapes=[
            vm((2 * rows, cols), BF16),
            vm((2, rows, width), F32),
            vm((2, width, rows), F32),
            vm((G, 2, R, rows), F32),
            vm((G, 4 * R, 2 * rows), BF16),
            vm((G, nz, R, CH), F32),
            vm((G, R, CH), F32),
            vm((G, 2 * R, rows), F32),
            vm((PH, G, nz, R, CH), F32),
            vm((PH, G, nz, R, CH), F32),
            vm((PH, G, nz, R, CH), BF16),
            vm((PH, G, nz, R, CH), BF16),
            vm((PH, G, 2, nz, R, CH), BF16),
            vm((ITERS, G, 2, 2 * R, rows), BF16),
            vm((ITERS, G, 2, 2 * R, rows), BF16),
            vm((G, 2, nz, 8, 128), F32),
            vm((PH, nx * ny, 8, 128), F32),
            vm((PH, 2 * nx, 8, 128), F32),
            vm((PH, nz, 8, 128), F32),
            vm((2 * nz, 8, 128), F32),
            sem((nz + 1,)),
            sem((PH,)),
            sem((PH, G, nz)), sem((PH, G, nz)),
            sem((PH, G, nz)), sem((PH, G, nz)),
            sem((PH, G, nz)), sem((PH, G, nz)),
            sem((PH, G, nz)), sem((PH, G, nz)),
            sem((ITERS, G, 2, 4)), sem((ITERS, G, 2, 4)),
            sem((PH, nx * ny)), sem((PH, nx * ny)),
            sem((PH, 2 * nx)), sem((PH, 2 * nx)),
            sem((PH, nz)), sem((PH, nz)),
            sem((2 * nz,)), sem((2 * nz,)),
        ],
        compiler_params=pltpu.CompilerParams(collective_id=0, has_side_effects=True, vmem_limit_bytes=56 << 20),
    )(kernel.reshape(2 * rows, cols), data[:, 0])
    out = jax.ShapeDtypeStruct((2, 1, cols, width), F32)

    def q_map(n):
        def index(i):
            me = lax.axis_index("rx") // 2
            return (0, 0, 0, lax.rem(i * FIN + n - me + nz, nz), 0, 0)

        return index

    out_spec = pl.BlockSpec((2, 1, FIN * CH, width), lambda i: (0, 0, i, 0))
    return pl.pallas_call(
        functools.partial(finish_kernel, dims),
        name="finish",
        grid=(nz // FIN,),
        out_shape=(out, out),
        in_specs=[pl.BlockSpec((PH, G, 2, 1, R, CH), q_map(n)) for n in range(FIN)]
        + [pl.BlockSpec((ITERS + PH, 8, 128), lambda i: (0, 0, 0))],
        out_specs=(out_spec, out_spec),
        scratch_shapes=[vm((FIN, 2, 2, width, CH), F32)],
        compiler_params=pltpu.CompilerParams(vmem_limit_bytes=60 << 20),
    )(*([q_all] * FIN), coefs)


def solution(mesh):
    nx, ny, nz = mesh.shape["freq"], mesh.shape["src"], mesh.shape["rx"] // 2
    return jax.shard_map(
        functools.partial(on_device, nx, ny, nz),
        mesh=mesh,
        in_specs=(P(None, "freq", "rx", "src"), P(None, "freq", "rx", None)),
        out_specs=(P(None, "freq", "src", None), P(None, "freq", "src", None)),
        check_vma=False,
    )
```

```python
import functools
import math

import jax
import jax.numpy as jnp
from jax import lax
from jax.experimental import pallas as pl
from jax.experimental.pallas import tpu as pltpu
from jax.sharding import PartitionSpec as P

GROUPS = 1
ITERS = 2
PH = ITERS + 1
CH = 256
MESH = pl.DeviceIdType.MESH
F32 = jnp.float32
BF16 = jnp.bfloat16
NN = (((1,), (0,)), ((), ()))
NT = (((1,), (1,)), ((), ()))


def tile_of_squares(x):
    sq = x * x
    rows, lanes = sq.shape
    part = jnp.sum(sq.reshape(rows // 8, 8, lanes), axis=0)
    total = part[:, :128]
    for i in range(1, lanes // 128):
        total = total + part[:, i * 128 : (i + 1) * 128]
    return total


def total_of(tile):
    return jnp.sum(tile, axis=(0, 1), keepdims=True)


FAR = (4, 3, 5, 2, 6, 1, 7, 0)
BATCHES = ((0, 1), (1, 2), (2, 3), (3, 5), (5, 8))
HILO = (True, True, False)


def lsqr_kernel(dims, g_hbm, data_hbm, x_out, w1_out, q2_out, coef_ref, g_v, data_ref, d_t, p_st, lhs, own, q_prev, acc, sib_s, sib_r, rs_s, rs_r,
                ag, y_s, y_r, nsq, sq_b, sp1_b, sp2_b, zc_b, out_buf, out_st, g_sem, out_sem, sib_ss, sib_rs, rs_ss, rs_rs, ag_ss, ag_rs,
                as_ss, as_rs, y_ss, y_rs, sq_ss, sq_rs, sp1_ss, sp1_rs, sp2_ss, sp2_rs, zc_ss, zc_rs):
    nx, ny, nz, rows, cols, width = dims
    half = width // 2
    vr = half // GROUPS
    R = 2 * vr
    hr = R // 2
    G = range(GROUPS)
    x = lax.axis_index("freq")
    y = lax.axis_index("src")
    rx = lax.axis_index("rx")
    me = rx // 2
    core = lax.rem(rx, 2)
    sib = {"rx": rx + 1 - 2 * core}
    zps = [{"rx": lax.rem(rx + 2 * o, 2 * nz)} for o in range(nz)]
    zcs = [{"rx": lax.rem(rx + 2 * o, 2 * nz) + 1 - 2 * core} for o in range(nz)]
    ynb = [{"src": y + 1 - 2 * lax.rem(y, 2)}, {"src": ny - 1 - y}]
    xps = [{"freq": lax.rem(x + o, nx)} for o in range(nx)]
    xcs = [{"freq": lax.rem(x + o, nx), "rx": rx + 1 - 2 * core} for o in range(nx)]
    xy = [(dx, dy) for dx in range(nx) for dy in range(ny) if dx or dy]
    xys = [{"freq": lax.rem(x + dx, nx), "src": lax.rem(y + dy, ny)} for dx, dy in xy]
    chunks = [lax.rem(me + o, nz) for o in range(nz)]
    lanes = [pl.ds(pl.multiple_of(c * CH, CH), CH) for c in chunks]

    started = []

    def rc(src, dst, ss, rs, dev):
        c = pltpu.make_async_remote_copy(src_ref=src, dst_ref=dst, send_sem=ss, recv_sem=rs, device_id=dev, device_id_type=MESH)
        c.start()
        started.append(c)

    def drain():
        for c in started:
            c.wait_send()
        started.clear()

    def wait_recv(dst, ss, rs):
        pltpu.make_async_remote_copy(src_ref=dst, dst_ref=dst, send_sem=ss, recv_sem=rs, device_id=sib, device_id_type=MESH).wait_recv()

    def g_copy(t):
        sl = lanes[FAR[t]]
        return pltpu.make_async_copy(g_hbm.at[:, sl], g_v.at[:, sl], g_sem.at[t])

    barrier = pltpu.get_barrier_semaphore()
    peers = zps[1:] + zcs + xys + xcs[1:]
    data_copy = pltpu.make_async_copy(data_hbm, data_ref, g_sem.at[nz])
    data_copy.start()
    for t in range(nz):
        g_copy(t).start()
    for p in peers:
        pl.semaphore_signal(barrier, inc=1, device_id=p, device_id_type=MESH)

    def tiles_send(buf, slot, tile, ss, rs, devs):
        buf[slot] = tile
        for i, dev in enumerate(devs):
            rc(buf.at[slot], buf.at[slot], ss.at[i], rs.at[slot], dev)

    def tiles_wait(buf, n, slots, ss, rs):
        for slot in slots:
            wait_recv(buf.at[slot], ss.at[0], rs.at[slot])
        tile = buf[0]
        for i in range(1, n):
            tile = tile + buf[i]
        return tile

    def sp1_send(k):
        tile = None
        for g in G:
            for pos in range(2):
                t = tile_of_squares(p_st[g, pos])
                tile = t if tile is None else tile + t
        tiles_send(sp1_b.at[k], 2 * x + core, tile, sp1_ss.at[k], sp1_rs.at[k], [sib] + xps[1:] + xcs[1:])

    def sp1_wait_sp2_send(k):
        slots = [2 * lax.rem(x + dx, nx) + lax.rem(core + dc, 2) for dx in range(nx) for dc in range(2) if dx or dc]
        tile = tiles_wait(sp1_b.at[k], 2 * nx, slots, sp1_ss.at[k], sp1_rs.at[k])
        tiles_send(sp2_b.at[k], me, tile, sp2_ss.at[k], sp2_rs.at[k], zps[1:])

    def sp2_wait(k):
        return jnp.sqrt(total_of(tiles_wait(sp2_b.at[k], nz, chunks[1:], sp2_ss.at[k], sp2_rs.at[k])))

    def sq_send(k):
        total = None
        for g in G:
            for pos in range(2):
                part = nsq[g, pos, 0]
                for ch in range(1, nz):
                    part = part + nsq[g, pos, ch]
                both = part if pos == 0 else both + part
            total = both if g == 0 else total + both
        tiles_send(sq_b.at[k], x * ny + y, total, sq_ss.at[k], sq_rs.at[k], xys)

    def sq_tile(k):
        slots = [lax.rem(x + dx, nx) * ny + lax.rem(y + dy, ny) for dx, dy in xy]
        return tiles_wait(sq_b.at[k], nx * ny, slots, sq_ss.at[k], sq_rs.at[k])

    def last_norm_send(k):
        total = None
        for g in G:
            t = tile_of_squares(ag[k, g, 0, 0].astype(F32))
            total = t if total is None else total + t
        tiles_send(sq_b.at[k], x * ny + y, total, sq_ss.at[k], sq_rs.at[k], xys)

    def last_norm_mid(k):
        tiles_send(zc_b, rx, sq_tile(k), zc_ss, zc_rs, zcs + zps[1:])

    def last_norm_wait():
        slots = [lax.rem(rx + d, 2 * nz) for d in range(1, 2 * nz)]
        return jnp.sqrt(total_of(tiles_wait(zc_b, 2 * nz, slots, zc_ss, zc_rs)))

    def build(k, g):
        for pos in range(2):
            u = p_st[g, pos]
            hi = u.astype(BF16)
            parts = (hi, (u - hi.astype(F32)).astype(BF16)) if HILO[k] else (hi,)
            for i, part in enumerate(parts):
                r0 = i * R
                lhs[g, pos, r0 : r0 + R, :rows] = part
                lhs[g, pos, r0 : r0 + vr, rows:] = part[vr:]
                lhs[g, pos, r0 + vr : r0 + R, rows:] = -part[:vr]

    def a1(k, g, batch, pos):
        t0, t1 = BATCHES[batch]
        for t in range(t0, t1):
            if k == 0 and g == 0 and pos == 1:
                g_copy(t).wait()
            if HILO[k]:
                res = lax.dot_general(lhs[g, pos], g_v[:, lanes[FAR[t]]], NN, preferred_element_type=F32)
                res = res[:R] + res[R:]
            else:
                res = lax.dot_general(lhs[g, pos, :R], g_v[:, lanes[FAR[t]]], NN, preferred_element_type=F32)
            if pos == 0:
                own[g, t] = res
            else:
                sib_s[k, g, t] = res
        if pos:
            part = pl.ds(t0, t1 - t0)
            rc(sib_s.at[k, g, part], sib_r.at[k, g, part], sib_ss.at[k, g, batch], sib_rs.at[k, g, batch], sib)

    def rs_send(k, g, slot, to, lo=0, n=R):
        part = pl.ds(lo, n)
        rc(rs_s.at[k, g, slot, part], rs_r.at[k, g, slot, part], rs_ss.at[k, g, slot], rs_rs.at[k, g, slot], zps[to])

    def rs_wait(k, g, slot, lo=0, n=R):
        part = pl.ds(lo, n)
        wait_recv(rs_r.at[k, g, slot, part], rs_ss.at[k, g, slot], rs_rs.at[k, g, slot])

    def a2(k, g, batch):
        t0, t1 = BATCHES[batch]
        part = pl.ds(t0, t1 - t0)
        wait_recv(sib_r.at[k, g, part], sib_ss.at[k, g, batch], sib_rs.at[k, g, batch])
        for t in range(t0, t1):
            off = FAR[t]
            pair = own[g, t] + sib_r[k, g, t]
            if off == 4:
                rs_s[k, g, 4, :hr] = pair[:hr].astype(BF16)
                rs_s[k, g, 0, hr:] = pair[hr:].astype(BF16)
                rs_send(k, g, 4, 2, 0, hr)
                rs_send(k, g, 0, nz - 2, hr, hr)
            elif off in (0, 2, nz - 2):
                own[g, t] = pair
            else:
                rs_s[k, g, off] = pair.astype(BF16)
                rs_send(k, g, off, 1 if off in (1, 3) else nz - 1)

    def a2b(k, g):
        rs_wait(k, g, 3)
        rs_wait(k, g, 4, 0, hr)
        s = own[g, FAR.index(2)] + rs_r[k, g, 3].astype(F32)
        rs_s[k, g, 2, :hr] = (s[:hr] + rs_r[k, g, 4, :hr].astype(F32)).astype(BF16)
        rs_s[k, g, 2, hr:] = s[hr:].astype(BF16)
        rs_send(k, g, 2, 2)
        rs_wait(k, g, nz - 3)
        rs_wait(k, g, 0, hr, hr)
        s = own[g, FAR.index(nz - 2)] + rs_r[k, g, nz - 3].astype(F32)
        rs_s[k, g, nz - 2, :hr] = s[:hr].astype(BF16)
        rs_s[k, g, nz - 2, hr:] = (s[hr:] + rs_r[k, g, 0, hr:].astype(F32)).astype(BF16)
        rs_send(k, g, nz - 2, nz - 2)

    def ag_send(k, g, rel, to, half=None):
        there = (rel - to) % nz
        rows_ = pl.ds(0, R) if half is None else pl.ds(half * hr, hr)
        sems = (k, g, half or 0, there)
        rc(ag.at[k, g, 0, rel, rows_], ag.at[k, g, 0, there, rows_], ag_ss.at[sems], ag_rs.at[sems], zps[to])

    def z_wait(k, g, rel, half=None):
        if rel in (1, nz - 1):
            wait_recv(ag.at[k, g, 0, rel], ag_ss.at[k, g, 0, rel], ag_rs.at[k, g, 0, rel])
            return
        for h in (0, 1) if half is None else (half,):
            wait_recv(ag.at[k, g, 0, rel, pl.ds(h * hr, hr)], ag_ss.at[k, g, h, rel], ag_rs.at[k, g, h, rel])

    def to_sib(k, g, rel, n=1):
        part = pl.ds(rel, n)
        rc(ag.at[k, g, 0, part], ag.at[k, g, 1, part], as_ss.at[k, g, rel], as_rs.at[k, g, rel], sib)

    def sib_wait(k, g, rel, n=1):
        part = pl.ds(rel, n)
        wait_recv(ag.at[k, g, 1, part], as_ss.at[k, g, rel], as_rs.at[k, g, rel])

    def a3(k, g, inv_beta, coef):
        s = own[g, FAR.index(0)]
        for off in (1, nz - 1, 2, nz - 2):
            rs_wait(k, g, off)
            s = s + rs_r[k, g, off].astype(F32)
        q = s * inv_beta
        if k:
            q = q - coef * q_prev[g]
        q_prev[g] = q
        ag[k, g, 0, 0] = q.astype(BF16)
        for to, h in ((nz - 2, 0), (2, 1), (nz - 2, 1), (2, 0)):
            ag_send(k, g, 0, to, h)
        for to in (1, nz - 1):
            ag_send(k, g, 0, to)
        to_sib(k, g, 0)

    def a4a(k, g):
        z_wait(k, g, 2, 0)
        ag_send(k, g, 2, nz - 2, 0)
        ag_send(k, g, 2, nz - 1, 0)
        z_wait(k, g, nz - 2, 1)
        ag_send(k, g, nz - 2, 2, 1)
        ag_send(k, g, nz - 2, 1, 1)
        z_wait(k, g, 2, 1)
        ag_send(k, g, 2, nz - 1, 1)
        z_wait(k, g, nz - 2, 0)
        ag_send(k, g, nz - 2, 1, 0)
        z_wait(k, g, 1)
        to_sib(k, g, 1, 2)
        z_wait(k, g, nz - 1)
        to_sib(k, g, nz - 2, 2)

    def a4b(k, g):
        for rel in (3, nz - 3, 4):
            z_wait(k, g, rel)
            to_sib(k, g, rel)

    def f1(k, g, rel, poss=(0, 1)):
        vs = [ag[k, g, pos, rel] for pos in poss]
        v = jnp.concatenate(vs, axis=0)
        w = jnp.concatenate([h for u in vs for h in (-u[vr:], u[:vr])], axis=0)
        res = lax.dot_general(v, g_v[:rows, lanes[rel]], NT, preferred_element_type=F32)
        res = res + lax.dot_general(w, g_v[rows:, lanes[rel]], NT, preferred_element_type=F32)
        sl = slice(poss[0] * R, (poss[-1] + 1) * R)
        if rel == 0:
            acc[g, sl] = res
        else:
            acc[g, sl] += res

    def q_norms(k, g, rel):
        for pos in range(2):
            nsq[g, pos, chunks[rel]] = tile_of_squares(ag[k, g, pos, rel].astype(F32))

    YP = [(pos, slice(pos * R + n * hr, pos * R + n * hr + hr), 2 * n + pos) for pos in range(2) for n in range(2)]

    def y_send(k, g, step, poss=(0, 1)):
        for pos, sl, i in YP:
            if pos not in poss:
                continue
            if step:
                wait_recv(y_r.at[k, g, 0, sl], y_ss.at[k, g, 0, i], y_rs.at[k, g, 0, i])
                acc[g, sl] = acc[g, sl] + y_r[k, g, 0, sl].astype(F32)
            y_s[k, g, step, sl] = acc[g, sl].astype(BF16)
            dev = ynb[(pos + step) % 2]
            rc(y_s.at[k, g, step, sl], y_r.at[k, g, step, sl], y_ss.at[k, g, step, i], y_rs.at[k, g, step, i], dev)

    def f2(k, g, inv_alpha, coef):
        for pos, sl, i in YP:
            wait_recv(y_r.at[k, g, 1, sl], y_ss.at[k, g, 1, i], y_rs.at[k, g, 1, i])
            total = acc[g, sl] + y_r[k, g, 1, sl].astype(F32)
            rs = slice(sl.start - pos * R, sl.stop - pos * R)
            p_st[g, pos, rs] = total * inv_alpha - coef * p_st[g, pos, rs]

    def out_copy(o, rel):
        dst = (x_out, w1_out, q2_out)[o].at[:, pl.ds(pl.multiple_of(chunks[rel] * CH, CH), CH)]
        return pltpu.make_async_copy(out_st.at[o, rel], dst, out_sem.at[o, rel])

    def out_chunk(o, rel, weights):
        for g in G:
            for pos in range(2):
                h = core if pos == 0 else 1 - core
                base = pl.multiple_of(h * half + g * vr, vr)
                if weights is None:
                    val = ag[ITERS, g, pos, rel]
                else:
                    val = sum(c * ag[j, g, pos, rel].astype(F32) for j, c in enumerate(weights)).astype(BF16)
                for c in range(2):
                    out_buf[o, rel, c, pl.ds(base, vr), :] = val[c * vr : (c + 1) * vr]
        for c in range(2):
            out_st[o, rel, c] = out_buf[o, rel, c].T
        out_copy(o, rel).start()

    recur = []

    def advance(beta, alpha=None):
        phibar, rhobar = recur_state[0]
        rho = jnp.sqrt(rhobar * rhobar + beta * beta)
        cosine, sine = rhobar / rho, beta / rho
        if alpha is None:
            return cosine * phibar / rho
        recur_state[0] = (sine * phibar, -cosine * alpha)
        recur.append((cosine * phibar / rho, sine * alpha / rho))

    recur_state = [None]

    data_copy.wait()
    for c in range(2):
        d_t[c] = data_ref[c].T
    for g in G:
        for pos in range(2):
            h = core if pos == 0 else 1 - core
            base = pl.multiple_of(h * half + g * vr, vr)
            for c in range(2):
                p_st[g, pos, c * vr : (c + 1) * vr, :] = d_t[c, pl.ds(base, vr), :]
    build(0, 0)
    pl.semaphore_wait(barrier, len(peers))

    alphas, betas = [], []
    for k in range(PH):
        last = k == ITERS
        for g in G:
            if k:
                f2(k - 1, g, inv_alpha, alphas[-1] / betas[-1])
            if k or g:
                build(k, g)
            for batch in (0, 1, 2):
                a1(k, g, batch, 1)
            for batch in (0, 1, 2):
                a1(k, g, batch, 0)
            if g == GROUPS - 1:
                sp1_send(k)
            for batch in (0, 1, 2):
                a2(k, g, batch)
        for g in G:
            for pos in (1, 0):
                for batch in (3, 4):
                    a1(k, g, batch, pos)
            a2(k, g, 3)
            a2(k, g, 4)
        if last:
            w_1 = (-recur[0][1] / alphas[0], 1.0 / alphas[1])
            for rel in range(nz):
                out_chunk(1, rel, w_1)
        sp1_wait_sp2_send(k)
        for g in G:
            a2b(k, g)
        betas.append(sp2_wait(k))
        inv_beta = 1.0 / betas[-1]
        coef = betas[-1] / alphas[-1] if k else None
        for g in G:
            a3(k, g, inv_beta, coef)
        if last:
            last_norm_send(k)
            step_2 = advance(betas[-1])
            x_w = ((recur[0][0] - step_2 * recur[0][1]) / alphas[0], step_2 / alphas[1])
            for rel in range(nz):
                out_chunk(0, rel, x_w)
            for g in G:
                a4a(k, g)
            last_norm_mid(k)
            for g in G:
                for rel, n in ((0, 1), (1, 2), (nz - 2, 2)):
                    sib_wait(k, g, rel, n)
            for rel in (0, 1, 2, nz - 2, nz - 1):
                out_chunk(2, rel, None)
            for g in G:
                a4b(k, g)
            drain()
            for rel in (3, nz - 3, 4):
                for g in G:
                    sib_wait(k, g, rel)
                out_chunk(2, rel, None)
            alphas.append(last_norm_wait())
            advance(betas[-1], alphas[-1])
            break
        for g in G:
            sib_wait(k, g, 0)
            f1(k, g, 0)
        for g in G:
            a4a(k, g)
        for g in G:
            sib_wait(k, g, 1, 2)
            f1(k, g, 1)
            f1(k, g, 2)
            sib_wait(k, g, nz - 2, 2)
            f1(k, g, nz - 2)
            f1(k, g, nz - 1)
        for g in G:
            for rel in (0, 1, 2, nz - 2, nz - 1):
                q_norms(k, g, rel)
        for g in G:
            for rel in (3, nz - 3, 4):
                z_wait(k, g, rel)
                to_sib(k, g, rel)
                f1(k, g, rel, (0,))
            y_send(k, g, 0, (0,))
        for g in G:
            for rel in (3, nz - 3, 4):
                sib_wait(k, g, rel)
                f1(k, g, rel, (1,))
            y_send(k, g, 0, (1,))
        for g in G:
            for rel in (3, nz - 3, 4):
                q_norms(k, g, rel)
        sq_send(k)
        for g in G:
            y_send(k, g, 1)
        drain()
        alphas.append(jnp.sqrt(total_of(sq_tile(k))))
        inv_alpha = 1.0 / alphas[-1]
        if k == 0:
            recur_state[0] = (betas[0], alphas[0])
        else:
            advance(betas[-1], alphas[-1])

    factor = math.sqrt(2.0 * nx * cols * ny * width)
    coef_ref[0] = jnp.broadcast_to(factor / alphas[-1], (8, 128))
    coef_ref[1] = jnp.broadcast_to(-factor * recur[-1][1], (8, 128))
    for o in range(3):
        for rel in range(nz):
            out_copy(o, rel).wait()


def finish_kernel(x_ref, w1_ref, q2_ref, coef_ref, x_out, w_out):
    for c in range(2):
        x_out[c, 0] = x_ref[c].astype(F32)
        w_out[c, 0] = q2_ref[c].astype(F32) * coef_ref[0, 0:1, 0:1] + w1_ref[c].astype(F32) * coef_ref[1, 0:1, 0:1]


def on_device(nx, ny, nz, kernel, data):
    rows, cols, width = kernel.shape[2], kernel.shape[3], data.shape[3]
    dims = (nx, ny, nz, rows, cols, width)
    R = width // GROUPS
    G = GROUPS
    sem = pltpu.SemaphoreType.DMA
    vm = pltpu.VMEM
    part = jax.ShapeDtypeStruct((2, cols, width), BF16)
    hbm = pl.BlockSpec(memory_space=pl.ANY)
    x_2, w_1, q_2, coefs = pl.pallas_call(
        functools.partial(lsqr_kernel, dims),
        name="lsqr",
        out_shape=(
            part,
            part,
            part,
            jax.ShapeDtypeStruct((2, 8, 128), F32),
        ),
        in_specs=[hbm, hbm],
        out_specs=(hbm, hbm, hbm, pl.BlockSpec(memory_space=pltpu.VMEM)),
        scratch_shapes=[
            vm((2 * rows, cols), BF16),
            vm((2, rows, width), F32),
            vm((2, width, rows), F32),
            vm((G, 2, R, rows), F32),
            vm((G, 2, 2 * R, 2 * rows), BF16),
            vm((G, nz, R, CH), F32),
            vm((G, R, CH), F32),
            vm((G, 2 * R, rows), F32),
            vm((PH, G, nz, R, CH), F32),
            vm((PH, G, nz, R, CH), F32),
            vm((PH, G, nz, R, CH), BF16),
            vm((PH, G, nz, R, CH), BF16),
            vm((PH, G, 2, nz, R, CH), BF16),
            vm((ITERS, G, 2, 2 * R, rows), BF16),
            vm((ITERS, G, 2, 2 * R, rows), BF16),
            vm((G, 2, nz, 8, 128), F32),
            vm((PH, nx * ny, 8, 128), F32),
            vm((PH, 2 * nx, 8, 128), F32),
            vm((PH, nz, 8, 128), F32),
            vm((2 * nz, 8, 128), F32),
            vm((3, nz, 2, width, CH), BF16),
            vm((3, nz, 2, CH, width), BF16),
            sem((nz + 1,)),
            sem((3, nz)),
            sem((PH, G, nz)), sem((PH, G, nz)),
            sem((PH, G, nz)), sem((PH, G, nz)),
            sem((PH, G, 2, nz)), sem((PH, G, 2, nz)),
            sem((PH, G, nz)), sem((PH, G, nz)),
            sem((ITERS, G, 2, 4)), sem((ITERS, G, 2, 4)),
            sem((PH, nx * ny)), sem((PH, nx * ny)),
            sem((PH, 2 * nx)), sem((PH, 2 * nx)),
            sem((PH, nz)), sem((PH, nz)),
            sem((2 * nz,)), sem((2 * nz,)),
        ],
        compiler_params=pltpu.CompilerParams(collective_id=0, has_side_effects=True, vmem_limit_bytes=56 << 20),
    )(kernel.reshape(2 * rows, cols), data[:, 0])
    out = jax.ShapeDtypeStruct((2, 1, cols, width), F32)
    blk = pl.BlockSpec((2, cols // 2, width), lambda i: (0, i, 0))
    out_blk = pl.BlockSpec((2, 1, cols // 2, width), lambda i: (0, 0, i, 0))
    return pl.pallas_call(
        finish_kernel,
        name="finish",
        grid=(2,),
        out_shape=(out, out),
        in_specs=[blk, blk, blk, pl.BlockSpec((2, 8, 128), lambda i: (0, 0, 0))],
        out_specs=(out_blk, out_blk),
        compiler_params=pltpu.CompilerParams(vmem_limit_bytes=60 << 20),
    )(x_2, w_1, q_2, coefs)


def solution(mesh):
    nx, ny, nz = mesh.shape["freq"], mesh.shape["src"], mesh.shape["rx"] // 2
    return jax.shard_map(
        functools.partial(on_device, nx, ny, nz),
        mesh=mesh,
        in_specs=(P(None, "freq", "rx", "src"), P(None, "freq", "rx", None)),
        out_specs=(P(None, "freq", "src", None), P(None, "freq", "src", None)),
        check_vma=False,
    )
```

```python
import functools
import math

import jax
import jax.numpy as jnp
from jax import lax
from jax.experimental import pallas as pl
from jax.experimental.pallas import tpu as pltpu
from jax.sharding import PartitionSpec as P

GROUPS = 1
ITERS = 2
PH = ITERS + 1
CH = 256
MESH = pl.DeviceIdType.MESH
F32 = jnp.float32
BF16 = jnp.bfloat16
NN = (((1,), (0,)), ((), ()))
NT = (((1,), (1,)), ((), ()))


def tile_of_squares(x):
    sq = x * x
    rows, lanes = sq.shape
    part = jnp.sum(sq.reshape(rows // 8, 8, lanes), axis=0)
    total = part[:, :128]
    for i in range(1, lanes // 128):
        total = total + part[:, i * 128 : (i + 1) * 128]
    return total


def total_of(tile):
    return jnp.sum(tile, axis=(0, 1), keepdims=True)


FAR = (4, 3, 5, 2, 6, 1, 7, 0)
BATCHES = ((0, 1), (1, 2), (2, 3), (3, 5), (5, 8))
HILO = (True, True, False)


def lsqr_kernel(dims, g_hbm, data_hbm, x_out, w1_out, q2_out, coef_ref, g_v, data_ref, d_t, p_st, lhs, own, q_prev, acc, sib_s, sib_r, rs_s, rs_r,
                ag, y_s, y_r, nsq, sq_b, sp1_b, sp2_b, zc_b, out_buf, out_st, g_sem, out_sem, send_sem, tile_rs, sib_rs, rs_rs,
                ag_rs, as_rs, y_rs):
    SIB, RS, AG, AS, Y, SQ, SP1, SP2, ZC = [send_sem.at[n] for n in range(9)]
    nx, ny, nz, rows, cols, width = dims
    half = width // 2
    vr = half // GROUPS
    R = 2 * vr
    hr = R // 2
    G = range(GROUPS)
    x = lax.axis_index("freq")
    y = lax.axis_index("src")
    rx = lax.axis_index("rx")
    me = rx // 2
    core = lax.rem(rx, 2)
    sib = {"rx": rx + 1 - 2 * core}
    zps = [{"rx": lax.rem(rx + 2 * o, 2 * nz)} for o in range(nz)]
    zcs = [{"rx": lax.rem(rx + 2 * o, 2 * nz) + 1 - 2 * core} for o in range(nz)]
    ynb = [{"src": y + 1 - 2 * lax.rem(y, 2)}, {"src": ny - 1 - y}]
    xps = [{"freq": lax.rem(x + o, nx)} for o in range(nx)]
    xcs = [{"freq": lax.rem(x + o, nx), "rx": rx + 1 - 2 * core} for o in range(nx)]
    xy = [(dx, dy) for dx in range(nx) for dy in range(ny) if dx or dy]
    xys = [{"freq": lax.rem(x + dx, nx), "src": lax.rem(y + dy, ny)} for dx, dy in xy]
    chunks = [lax.rem(me + o, nz) for o in range(nz)]
    lanes = [pl.ds(pl.multiple_of(c * CH, CH), CH) for c in chunks]

    def rc(src, dst, ss, rs, dev):
        pltpu.make_async_remote_copy(src_ref=src, dst_ref=dst, send_sem=ss, recv_sem=rs, device_id=dev, device_id_type=MESH).start()

    def wait_recv(dst, rs):
        pltpu.make_async_remote_copy(src_ref=dst, dst_ref=dst, send_sem=SIB, recv_sem=rs, device_id=sib, device_id_type=MESH).wait_recv()

    def wait_sent(src, ss):
        pltpu.make_async_remote_copy(src_ref=src, dst_ref=src, send_sem=ss, recv_sem=tile_rs.at[0], device_id=sib, device_id_type=MESH).wait_send()

    def drain(k):
        for g in G:
            wait_sent(sib_s.at[k, g], SIB)
            wait_sent(rs_s.at[k, g, pl.ds(1, nz - 1)], RS)
            wait_sent(ag.at[k, g, 0, pl.ds(1, nz - 1)], AG)
            wait_sent(ag.at[k, g, 0], AS)
            if k < ITERS:
                wait_sent(y_s.at[k, g], Y)
        wait_sent(sq_b.at[k, pl.ds(1, nx * ny - 1)], SQ)
        wait_sent(sp1_b.at[k, pl.ds(1, 2 * nx - 1)], SP1)
        wait_sent(sp2_b.at[k, pl.ds(1, nz - 1)], SP2)
        if k == ITERS:
            wait_sent(zc_b.at[pl.ds(1, 2 * nz - 1)], ZC)

    def g_copy(t):
        sl = lanes[FAR[t]]
        return pltpu.make_async_copy(g_hbm.at[:, sl], g_v.at[:, sl], g_sem.at[t])

    barrier = pltpu.get_barrier_semaphore()
    peers = zps[1:] + zcs + xys + xcs[1:]
    data_copy = pltpu.make_async_copy(data_hbm, data_ref, g_sem.at[nz])
    data_copy.start()
    for t in range(nz):
        g_copy(t).start()
    for p in peers:
        pl.semaphore_signal(barrier, inc=1, device_id=p, device_id_type=MESH)

    def tiles_send(buf, slot, tile, ss, rs, devs):
        buf[slot] = tile
        for dev in devs:
            rc(buf.at[slot], buf.at[slot], ss, rs, dev)

    def tiles_wait(buf, n, rs):
        wait_recv(buf.at[pl.ds(1, n - 1)], rs)
        tile = buf[0]
        for i in range(1, n):
            tile = tile + buf[i]
        return tile

    def sp1_send(k):
        tile = None
        for g in G:
            for pos in range(2):
                t = tile_of_squares(p_st[g, pos])
                tile = t if tile is None else tile + t
        tiles_send(sp1_b.at[k], 2 * x + core, tile, SP1, tile_rs.at[PH + k], [sib] + xps[1:] + xcs[1:])

    def sp1_wait_sp2_send(k):
        tile = tiles_wait(sp1_b.at[k], 2 * nx, tile_rs.at[PH + k])
        tiles_send(sp2_b.at[k], me, tile, SP2, tile_rs.at[2 * PH + k], zps[1:])

    def sp2_wait(k):
        return jnp.sqrt(total_of(tiles_wait(sp2_b.at[k], nz, tile_rs.at[2 * PH + k])))

    def sq_send(k):
        total = None
        for g in G:
            for pos in range(2):
                part = nsq[g, pos, 0]
                for ch in range(1, nz):
                    part = part + nsq[g, pos, ch]
                both = part if pos == 0 else both + part
            total = both if g == 0 else total + both
        tiles_send(sq_b.at[k], x * ny + y, total, SQ, tile_rs.at[k], xys)

    def sq_tile(k):
        return tiles_wait(sq_b.at[k], nx * ny, tile_rs.at[k])

    def last_norm_send(k):
        total = None
        for g in G:
            t = tile_of_squares(ag[k, g, 0, 0].astype(F32))
            total = t if total is None else total + t
        tiles_send(sq_b.at[k], x * ny + y, total, SQ, tile_rs.at[k], xys)

    def last_norm_mid(k):
        tiles_send(zc_b, rx, sq_tile(k), ZC, tile_rs.at[3 * PH], zcs + zps[1:])

    def last_norm_wait():
        return jnp.sqrt(total_of(tiles_wait(zc_b, 2 * nz, tile_rs.at[3 * PH])))

    def build(k, g):
        for pos in range(2):
            u = p_st[g, pos]
            hi = u.astype(BF16)
            parts = (hi, (u - hi.astype(F32)).astype(BF16)) if HILO[k] else (hi,)
            for i, part in enumerate(parts):
                r0 = i * R
                lhs[g, pos, r0 : r0 + R, :rows] = part
                lhs[g, pos, r0 : r0 + vr, rows:] = part[vr:]
                lhs[g, pos, r0 + vr : r0 + R, rows:] = -part[:vr]

    def a1(k, g, batch, pos):
        t0, t1 = BATCHES[batch]
        for t in range(t0, t1):
            if k == 0 and g == 0 and pos == 1:
                g_copy(t).wait()
            if HILO[k]:
                res = lax.dot_general(lhs[g, pos], g_v[:, lanes[FAR[t]]], NN, preferred_element_type=F32)
                res = res[:R] + res[R:]
            else:
                res = lax.dot_general(lhs[g, pos, :R], g_v[:, lanes[FAR[t]]], NN, preferred_element_type=F32)
            if pos == 0:
                own[g, t] = res
            else:
                sib_s[k, g, t] = res

    def sib_send(k, g, batch):
        t0, t1 = BATCHES[batch]
        part = pl.ds(t0, t1 - t0)
        rc(sib_s.at[k, g, part], sib_r.at[k, g, part], SIB, sib_rs.at[k, g, batch], sib)

    def rs_send(k, g, slot, to, lo=0, n=R):
        part = pl.ds(lo, n)
        rc(rs_s.at[k, g, slot, part], rs_r.at[k, g, slot, part], RS, rs_rs.at[k, g, slot], zps[to])

    def rs_wait(k, g, slot, lo=0, n=R):
        part = pl.ds(lo, n)
        wait_recv(rs_r.at[k, g, slot, part], rs_rs.at[k, g, slot])

    def a2(k, g, batch):
        t0, t1 = BATCHES[batch]
        part = pl.ds(t0, t1 - t0)
        wait_recv(sib_r.at[k, g, part], sib_rs.at[k, g, batch])
        for t in range(t0, t1):
            off = FAR[t]
            pair = own[g, t] + sib_r[k, g, t]
            if off == 4:
                rs_s[k, g, 4, :hr] = pair[:hr].astype(BF16)
                rs_s[k, g, 0, hr:] = pair[hr:].astype(BF16)
                rs_send(k, g, 4, 2, 0, hr)
                rs_send(k, g, 0, nz - 2, hr, hr)
            elif off in (0, 2, nz - 2):
                own[g, t] = pair
            else:
                rs_s[k, g, off] = pair.astype(BF16)
                rs_send(k, g, off, 1 if off in (1, 3) else nz - 1)

    def a2b(k, g):
        rs_wait(k, g, 3)
        rs_wait(k, g, 4, 0, hr)
        s = own[g, FAR.index(2)] + rs_r[k, g, 3].astype(F32)
        rs_s[k, g, 2, :hr] = (s[:hr] + rs_r[k, g, 4, :hr].astype(F32)).astype(BF16)
        rs_s[k, g, 2, hr:] = s[hr:].astype(BF16)
        rs_send(k, g, 2, 2)
        rs_wait(k, g, nz - 3)
        rs_wait(k, g, 0, hr, hr)
        s = own[g, FAR.index(nz - 2)] + rs_r[k, g, nz - 3].astype(F32)
        rs_s[k, g, nz - 2, :hr] = s[:hr].astype(BF16)
        rs_s[k, g, nz - 2, hr:] = (s[hr:] + rs_r[k, g, 0, hr:].astype(F32)).astype(BF16)
        rs_send(k, g, nz - 2, nz - 2)

    def ag_sem(k, g, rel, half):
        return ag_rs.at[k, g, {(2, 1): 0, (nz - 2, 0): nz}.get((rel, half), rel)]

    def ag_send(k, g, rel, to, half=None):
        there = (rel - to) % nz
        part = pl.ds(0, R) if half is None else pl.ds(half * hr, hr)
        rc(ag.at[k, g, 0, rel, part], ag.at[k, g, 0, there, part], AG, ag_sem(k, g, there, half), zps[to])

    def z_wait(k, g, rel, half=None):
        part = pl.ds(0, R) if half is None else pl.ds(half * hr, hr)
        wait_recv(ag.at[k, g, 0, rel, part], ag_sem(k, g, rel, half))

    def to_sib(k, g, rel, n=1):
        part = pl.ds(rel, n)
        rc(ag.at[k, g, 0, part], ag.at[k, g, 1, part], AS, as_rs.at[k, g, rel], sib)

    def sib_wait(k, g, rel, n=1):
        part = pl.ds(rel, n)
        wait_recv(ag.at[k, g, 1, part], as_rs.at[k, g, rel])

    def a3(k, g, inv_beta, coef):
        s = own[g, FAR.index(0)]
        for off in (1, nz - 1, 2, nz - 2):
            rs_wait(k, g, off)
            s = s + rs_r[k, g, off].astype(F32)
        q = s * inv_beta
        if k:
            q = q - coef * q_prev[g]
        q_prev[g] = q
        ag[k, g, 0, 0] = q.astype(BF16)
        for to, h in ((nz - 2, 0), (2, 1), (nz - 2, 1), (2, 0)):
            ag_send(k, g, 0, to, h)
        for to in (1, nz - 1):
            ag_send(k, g, 0, to)
        to_sib(k, g, 0)

    def a4a(k, g):
        z_wait(k, g, 2, 0)
        ag_send(k, g, 2, nz - 2, 0)
        ag_send(k, g, 2, nz - 1, 0)
        z_wait(k, g, nz - 2, 1)
        ag_send(k, g, nz - 2, 2, 1)
        ag_send(k, g, nz - 2, 1, 1)
        z_wait(k, g, 2, 1)
        ag_send(k, g, 2, nz - 1, 1)
        z_wait(k, g, nz - 2, 0)
        ag_send(k, g, nz - 2, 1, 0)
        z_wait(k, g, 1)
        to_sib(k, g, 1, 2)
        z_wait(k, g, nz - 1)
        to_sib(k, g, nz - 2, 2)

    def a4b(k, g):
        for rel in (3, nz - 3, 4):
            z_wait(k, g, rel)
            to_sib(k, g, rel)

    def f1(k, g, rel, poss=(0, 1)):
        vs = [ag[k, g, pos, rel] for pos in poss]
        v = jnp.concatenate(vs, axis=0)
        w = jnp.concatenate([h for u in vs for h in (-u[vr:], u[:vr])], axis=0)
        res = lax.dot_general(v, g_v[:rows, lanes[rel]], NT, preferred_element_type=F32)
        res = res + lax.dot_general(w, g_v[rows:, lanes[rel]], NT, preferred_element_type=F32)
        sl = slice(poss[0] * R, (poss[-1] + 1) * R)
        if rel == 0:
            acc[g, sl] = res
        else:
            acc[g, sl] += res

    def q_norms(k, g, rel):
        for pos in range(2):
            nsq[g, pos, chunks[rel]] = tile_of_squares(ag[k, g, pos, rel].astype(F32))

    YP = [(pos, slice(pos * R + n * hr, pos * R + n * hr + hr), 2 * n + pos) for pos in range(2) for n in range(2)]

    def y_send(k, g, step, poss=(0, 1)):
        for pos, sl, i in YP:
            if pos not in poss:
                continue
            if step:
                wait_recv(y_r.at[k, g, 0, sl], y_rs.at[k, g, 0, i])
                acc[g, sl] = acc[g, sl] + y_r[k, g, 0, sl].astype(F32)
            y_s[k, g, step, sl] = acc[g, sl].astype(BF16)
            dev = ynb[(pos + step) % 2]
            rc(y_s.at[k, g, step, sl], y_r.at[k, g, step, sl], Y, y_rs.at[k, g, step, i], dev)

    def f2(k, g, inv_alpha, coef):
        for pos, sl, i in YP:
            wait_recv(y_r.at[k, g, 1, sl], y_rs.at[k, g, 1, i])
            total = acc[g, sl] + y_r[k, g, 1, sl].astype(F32)
            rs = slice(sl.start - pos * R, sl.stop - pos * R)
            p_st[g, pos, rs] = total * inv_alpha - coef * p_st[g, pos, rs]

    def out_copy(o, rel):
        dst = (x_out, w1_out, q2_out)[o].at[:, pl.ds(pl.multiple_of(chunks[rel] * CH, CH), CH)]
        return pltpu.make_async_copy(out_st.at[o, rel], dst, out_sem.at[o])

    def out_chunk(o, rel, weights):
        for g in G:
            for pos in range(2):
                h = core if pos == 0 else 1 - core
                base = pl.multiple_of(h * half + g * vr, vr)
                if weights is None:
                    val = ag[ITERS, g, pos, rel]
                else:
                    val = sum(c * ag[j, g, pos, rel].astype(F32) for j, c in enumerate(weights)).astype(BF16)
                for c in range(2):
                    out_buf[o, rel, c, pl.ds(base, vr), :] = val[c * vr : (c + 1) * vr]
        for c in range(2):
            out_st[o, rel, c] = out_buf[o, rel, c].T
        out_copy(o, rel).start()

    recur = []

    def advance(beta, alpha=None):
        phibar, rhobar = recur_state[0]
        rho = jnp.sqrt(rhobar * rhobar + beta * beta)
        cosine, sine = rhobar / rho, beta / rho
        if alpha is None:
            return cosine * phibar / rho
        recur_state[0] = (sine * phibar, -cosine * alpha)
        recur.append((cosine * phibar / rho, sine * alpha / rho))

    recur_state = [None]

    data_copy.wait()
    for c in range(2):
        d_t[c] = data_ref[c].T
    for g in G:
        for pos in range(2):
            h = core if pos == 0 else 1 - core
            base = pl.multiple_of(h * half + g * vr, vr)
            for c in range(2):
                p_st[g, pos, c * vr : (c + 1) * vr, :] = d_t[c, pl.ds(base, vr), :]
    build(0, 0)

    alphas, betas = [], []
    for k in range(PH):
        last = k == ITERS
        for g in G:
            if k:
                f2(k - 1, g, inv_alpha, alphas[-1] / betas[-1])
            if k or g:
                build(k, g)
            if k == 0:
                for pos in (1, 0):
                    for batch in range(5):
                        a1(k, g, batch, pos)
                if g == 0:
                    pl.semaphore_wait(barrier, len(peers))
                for batch in range(5):
                    sib_send(k, g, batch)
            else:
                for batch in (0, 1, 2):
                    a1(k, g, batch, 1)
                    sib_send(k, g, batch)
                for batch in (0, 1, 2):
                    a1(k, g, batch, 0)
            if g == GROUPS - 1:
                sp1_send(k)
            for batch in (0, 1, 2):
                a2(k, g, batch)
        for g in G:
            if k:
                for batch in (3, 4):
                    a1(k, g, batch, 1)
                    sib_send(k, g, batch)
                for batch in (3, 4):
                    a1(k, g, batch, 0)
            a2(k, g, 3)
            a2(k, g, 4)
        if last:
            w_1 = (-recur[0][1] / alphas[0], 1.0 / alphas[1])
            for rel in range(nz):
                out_chunk(1, rel, w_1)
        sp1_wait_sp2_send(k)
        for g in G:
            a2b(k, g)
        betas.append(sp2_wait(k))
        inv_beta = 1.0 / betas[-1]
        coef = betas[-1] / alphas[-1] if k else None
        for g in G:
            a3(k, g, inv_beta, coef)
        if last:
            last_norm_send(k)
            step_2 = advance(betas[-1])
            x_w = ((recur[0][0] - step_2 * recur[0][1]) / alphas[0], step_2 / alphas[1])
            for rel in range(nz):
                out_chunk(0, rel, x_w)
            for g in G:
                a4a(k, g)
            last_norm_mid(k)
            for g in G:
                for rel, n in ((0, 1), (1, 2), (nz - 2, 2)):
                    sib_wait(k, g, rel, n)
            for rel in (0, 1, 2, nz - 2, nz - 1):
                out_chunk(2, rel, None)
            for g in G:
                a4b(k, g)
            for rel in (3, nz - 3, 4):
                for g in G:
                    sib_wait(k, g, rel)
                out_chunk(2, rel, None)
            alphas.append(last_norm_wait())
            drain(k)
            advance(betas[-1], alphas[-1])
            break
        for g in G:
            sib_wait(k, g, 0)
            f1(k, g, 0)
        for g in G:
            a4a(k, g)
        for g in G:
            sib_wait(k, g, 1, 2)
            f1(k, g, 1)
            f1(k, g, 2)
            sib_wait(k, g, nz - 2, 2)
            f1(k, g, nz - 2)
            f1(k, g, nz - 1)
        for g in G:
            for rel in (0, 1, 2, nz - 2, nz - 1):
                q_norms(k, g, rel)
        for g in G:
            for rel in (3, nz - 3, 4):
                z_wait(k, g, rel)
                to_sib(k, g, rel)
                f1(k, g, rel, (0,))
            y_send(k, g, 0, (0,))
        for g in G:
            for rel in (3, nz - 3, 4):
                sib_wait(k, g, rel)
                f1(k, g, rel, (1,))
            y_send(k, g, 0, (1,))
        for g in G:
            for rel in (3, nz - 3, 4):
                q_norms(k, g, rel)
        sq_send(k)
        for g in G:
            y_send(k, g, 1)
        drain(k)
        alphas.append(jnp.sqrt(total_of(sq_tile(k))))
        inv_alpha = 1.0 / alphas[-1]
        if k == 0:
            recur_state[0] = (betas[0], alphas[0])
        else:
            advance(betas[-1], alphas[-1])

    factor = math.sqrt(2.0 * nx * cols * ny * width)
    coef_ref[0] = jnp.broadcast_to(factor / alphas[-1], (8, 128))
    coef_ref[1] = jnp.broadcast_to(-factor * recur[-1][1], (8, 128))
    for o in range(3):
        pltpu.make_async_copy(out_st.at[o], out_st.at[o], out_sem.at[o]).wait()


def finish_kernel(x_ref, w1_ref, q2_ref, coef_ref, x_out, w_out):
    for c in range(2):
        x_out[c, 0] = x_ref[c].astype(F32)
        w_out[c, 0] = q2_ref[c].astype(F32) * coef_ref[0, 0:1, 0:1] + w1_ref[c].astype(F32) * coef_ref[1, 0:1, 0:1]


def on_device(nx, ny, nz, kernel, data):
    rows, cols, width = kernel.shape[2], kernel.shape[3], data.shape[3]
    dims = (nx, ny, nz, rows, cols, width)
    R = width // GROUPS
    G = GROUPS
    sem = pltpu.SemaphoreType.DMA
    vm = pltpu.VMEM
    part = jax.ShapeDtypeStruct((2, cols, width), BF16)
    hbm = pl.BlockSpec(memory_space=pl.ANY)
    x_2, w_1, q_2, coefs = pl.pallas_call(
        functools.partial(lsqr_kernel, dims),
        name="lsqr",
        out_shape=(
            part,
            part,
            part,
            jax.ShapeDtypeStruct((2, 8, 128), F32),
        ),
        in_specs=[hbm, hbm],
        out_specs=(hbm, hbm, hbm, pl.BlockSpec(memory_space=pltpu.VMEM)),
        scratch_shapes=[
            vm((2 * rows, cols), BF16),
            vm((2, rows, width), F32),
            vm((2, width, rows), F32),
            vm((G, 2, R, rows), F32),
            vm((G, 2, 2 * R, 2 * rows), BF16),
            vm((G, nz, R, CH), F32),
            vm((G, R, CH), F32),
            vm((G, 2 * R, rows), F32),
            vm((PH, G, nz, R, CH), F32),
            vm((PH, G, nz, R, CH), F32),
            vm((PH, G, nz, R, CH), BF16),
            vm((PH, G, nz, R, CH), BF16),
            vm((PH, G, 2, nz, R, CH), BF16),
            vm((ITERS, G, 2, 2 * R, rows), BF16),
            vm((ITERS, G, 2, 2 * R, rows), BF16),
            vm((G, 2, nz, 8, 128), F32),
            vm((PH, nx * ny, 8, 128), F32),
            vm((PH, 2 * nx, 8, 128), F32),
            vm((PH, nz, 8, 128), F32),
            vm((2 * nz, 8, 128), F32),
            vm((3, nz, 2, width, CH), BF16),
            vm((3, nz, 2, CH, width), BF16),
            sem((nz + 1,)),
            sem((3,)),
            sem((9,)),
            sem((3 * PH + 1,)),
            sem((PH, G, 5)),
            sem((PH, G, nz)),
            sem((PH, G, nz + 1)),
            sem((PH, G, nz)),
            sem((ITERS, G, 2, 4)),
        ],
        compiler_params=pltpu.CompilerParams(collective_id=0, has_side_effects=True, vmem_limit_bytes=56 << 20),
    )(kernel.reshape(2 * rows, cols), data[:, 0])
    out = jax.ShapeDtypeStruct((2, 1, cols, width), F32)
    blk = pl.BlockSpec((2, cols // 2, width), lambda i: (0, i, 0))
    out_blk = pl.BlockSpec((2, 1, cols // 2, width), lambda i: (0, 0, i, 0))
    return pl.pallas_call(
        finish_kernel,
        name="finish",
        grid=(2,),
        out_shape=(out, out),
        in_specs=[blk, blk, blk, pl.BlockSpec((2, 8, 128), lambda i: (0, 0, 0))],
        out_specs=(out_blk, out_blk),
        compiler_params=pltpu.CompilerParams(vmem_limit_bytes=60 << 20),
    )(x_2, w_1, q_2, coefs)


def solution(mesh):
    nx, ny, nz = mesh.shape["freq"], mesh.shape["src"], mesh.shape["rx"] // 2
    return jax.shard_map(
        functools.partial(on_device, nx, ny, nz),
        mesh=mesh,
        in_specs=(P(None, "freq", "rx", "src"), P(None, "freq", "rx", None)),
        out_specs=(P(None, "freq", "src", None), P(None, "freq", "src", None)),
        check_vma=False,
    )
```

```python
import functools
import math

import jax
import jax.numpy as jnp
from jax import lax
from jax.experimental import pallas as pl
from jax.experimental.pallas import tpu as pltpu
from jax.sharding import PartitionSpec as P

GROUPS = 1
ITERS = 2
PH = ITERS + 1
CH = 256
MESH = pl.DeviceIdType.MESH
F32 = jnp.float32
BF16 = jnp.bfloat16
NN = (((1,), (0,)), ((), ()))
NT = (((1,), (1,)), ((), ()))


def tile_of_squares(x):
    sq = x * x
    rows, lanes = sq.shape
    part = jnp.sum(sq.reshape(rows // 8, 8, lanes), axis=0)
    total = part[:, :128]
    for i in range(1, lanes // 128):
        total = total + part[:, i * 128 : (i + 1) * 128]
    return total


def total_of(tile):
    return jnp.sum(tile, axis=(0, 1), keepdims=True)


FAR = (4, 3, 5, 2, 6, 1, 7, 0)
BATCHES = ((0, 1), (1, 2), (2, 3), (3, 5), (5, 8))
HILO = (True, True, False)


def lsqr_kernel(dims, g_hbm, data_hbm, x_out, w1_out, q2_out, coef_ref, g_v, data_ref, d_t, p_st, lhs, own, q_prev, acc, sib_s, sib_r, rs_s, rs_r,
                ag, y_s, y_r, nsq, sq_b, sp1_b, sp2_b, zc_b, out_buf, out_st, g_sem, out_sem, send_sem, tile_rs, sib_rs, rs_rs,
                ag_rs, as_rs, y_rs):
    SIB, RS, AG, AS, Y, SQ, SP1, SP2, ZC = [send_sem.at[n] for n in range(9)]
    nx, ny, nz, rows, cols, width = dims
    half = width // 2
    vr = half // GROUPS
    R = 2 * vr
    hr = R // 2
    G = range(GROUPS)
    x = lax.axis_index("freq")
    y = lax.axis_index("src")
    rx = lax.axis_index("rx")
    me = rx // 2
    core = lax.rem(rx, 2)
    sib = {"rx": rx + 1 - 2 * core}
    zps = [{"rx": lax.rem(rx + 2 * o, 2 * nz)} for o in range(nz)]
    zcs = [{"rx": lax.rem(rx + 2 * o, 2 * nz) + 1 - 2 * core} for o in range(nz)]
    ynb = [{"src": y + 1 - 2 * lax.rem(y, 2)}, {"src": ny - 1 - y}]
    xps = [{"freq": lax.rem(x + o, nx)} for o in range(nx)]
    xcs = [{"freq": lax.rem(x + o, nx), "rx": rx + 1 - 2 * core} for o in range(nx)]
    xy = [(dx, dy) for dx in range(nx) for dy in range(ny) if dx or dy]
    xys = [{"freq": lax.rem(x + dx, nx), "src": lax.rem(y + dy, ny)} for dx, dy in xy]
    chunks = [lax.rem(me + o, nz) for o in range(nz)]
    lanes = [pl.ds(pl.multiple_of(c * CH, CH), CH) for c in chunks]

    def rc(src, dst, ss, rs, dev):
        pltpu.make_async_remote_copy(src_ref=src, dst_ref=dst, send_sem=ss, recv_sem=rs, device_id=dev, device_id_type=MESH).start()

    def wait_recv(dst, rs):
        pltpu.make_async_remote_copy(src_ref=dst, dst_ref=dst, send_sem=SIB, recv_sem=rs, device_id=sib, device_id_type=MESH).wait_recv()

    def wait_sent(src, ss):
        pltpu.make_async_remote_copy(src_ref=src, dst_ref=src, send_sem=ss, recv_sem=tile_rs.at[0], device_id=sib, device_id_type=MESH).wait_send()

    def drain(k):
        for g in G:
            wait_sent(sib_s.at[k, g], SIB)
            wait_sent(rs_s.at[k, g, pl.ds(1, nz - 1)], RS)
            wait_sent(ag.at[k, g, 0, pl.ds(1, nz - 1)], AG)
            wait_sent(ag.at[k, g, 0], AS)
            if k < ITERS:
                wait_sent(y_s.at[k, g], Y)
        wait_sent(sq_b.at[k, pl.ds(1, nx * ny - 1)], SQ)
        wait_sent(sp1_b.at[k, pl.ds(1, 2 * nx - 1)], SP1)
        wait_sent(sp2_b.at[k, pl.ds(1, nz - 1)], SP2)
        if k == ITERS:
            wait_sent(zc_b.at[pl.ds(1, 2 * nz - 1)], ZC)

    def g_copy(t):
        sl = lanes[FAR[t]]
        return pltpu.make_async_copy(g_hbm.at[:, sl], g_v.at[:, sl], g_sem.at[t])

    barrier = pltpu.get_barrier_semaphore()
    peers = zps[1:] + zcs + xys + xcs[1:]
    data_copy = pltpu.make_async_copy(data_hbm, data_ref, g_sem.at[nz])
    data_copy.start()
    for t in range(nz):
        g_copy(t).start()
    for p in peers:
        pl.semaphore_signal(barrier, inc=1, device_id=p, device_id_type=MESH)

    def tiles_send(buf, slot, tile, ss, rs, devs):
        buf[slot] = tile
        for dev in devs:
            rc(buf.at[slot], buf.at[slot], ss, rs, dev)

    def tiles_wait(buf, n, rs):
        wait_recv(buf.at[pl.ds(1, n - 1)], rs)
        tile = buf[0]
        for i in range(1, n):
            tile = tile + buf[i]
        return tile

    def sp1_send(k):
        tile = None
        for g in G:
            for pos in range(2):
                t = tile_of_squares(p_st[g, pos])
                tile = t if tile is None else tile + t
        tiles_send(sp1_b.at[k], 2 * x + core, tile, SP1, tile_rs.at[PH + k], [sib] + xps[1:] + xcs[1:])

    def sp1_wait_sp2_send(k):
        tile = tiles_wait(sp1_b.at[k], 2 * nx, tile_rs.at[PH + k])
        tiles_send(sp2_b.at[k], me, tile, SP2, tile_rs.at[2 * PH + k], zps[1:])

    def sp2_wait(k):
        return jnp.sqrt(total_of(tiles_wait(sp2_b.at[k], nz, tile_rs.at[2 * PH + k])))

    def sq_send(k):
        total = None
        for g in G:
            for pos in range(2):
                part = nsq[g, pos, 0]
                for ch in range(1, nz):
                    part = part + nsq[g, pos, ch]
                both = part if pos == 0 else both + part
            total = both if g == 0 else total + both
        tiles_send(sq_b.at[k], x * ny + y, total, SQ, tile_rs.at[k], xys)

    def sq_tile(k):
        return tiles_wait(sq_b.at[k], nx * ny, tile_rs.at[k])

    def last_norm_send(k):
        total = None
        for g in G:
            t = tile_of_squares(ag[k, g, 0, 0].astype(F32))
            total = t if total is None else total + t
        tiles_send(sq_b.at[k], x * ny + y, total, SQ, tile_rs.at[k], xys)

    def last_norm_mid(k):
        tiles_send(zc_b, rx, sq_tile(k), ZC, tile_rs.at[3 * PH], zcs + zps[1:])

    def last_norm_wait():
        return jnp.sqrt(total_of(tiles_wait(zc_b, 2 * nz, tile_rs.at[3 * PH])))

    def build(k, g):
        for pos in range(2):
            u = p_st[g, pos]
            hi = u.astype(BF16)
            parts = (hi, (u - hi.astype(F32)).astype(BF16)) if HILO[k] else (hi,)
            for i, part in enumerate(parts):
                r0 = i * R
                lhs[g, pos, r0 : r0 + R, :rows] = part
                lhs[g, pos, r0 : r0 + vr, rows:] = part[vr:]
                lhs[g, pos, r0 + vr : r0 + R, rows:] = -part[:vr]

    def a1(k, g, batch, pos):
        t0, t1 = BATCHES[batch]
        for t in range(t0, t1):
            if k == 0 and g == 0 and pos == 1:
                g_copy(t).wait()
            if HILO[k]:
                res = lax.dot_general(lhs[g, pos], g_v[:, lanes[FAR[t]]], NN, preferred_element_type=F32)
                res = res[:R] + res[R:]
            else:
                res = lax.dot_general(lhs[g, pos, :R], g_v[:, lanes[FAR[t]]], NN, preferred_element_type=F32)
            if pos == 0:
                own[g, t] = res
            else:
                sib_s[k, g, t] = res

    def sib_send(k, g, batch):
        t0, t1 = BATCHES[batch]
        part = pl.ds(t0, t1 - t0)
        rc(sib_s.at[k, g, part], sib_r.at[k, g, part], SIB, sib_rs.at[k, g, batch], sib)

    def rs_send(k, g, slot, to, half=None):
        part = pl.ds(0, R) if half is None else pl.ds(half * hr, hr)
        rc(rs_s.at[k, g, slot, part], rs_r.at[k, g, slot, part], RS, rs_rs.at[k, g, half or 0, slot], zps[to])

    def rs_wait(k, g, slot, half=None):
        part = pl.ds(0, R) if half is None else pl.ds(half * hr, hr)
        wait_recv(rs_r.at[k, g, slot, part], rs_rs.at[k, g, half or 0, slot])

    def a2(k, g, batch):
        t0, t1 = BATCHES[batch]
        part = pl.ds(t0, t1 - t0)
        wait_recv(sib_r.at[k, g, part], sib_rs.at[k, g, batch])
        for t in range(t0, t1):
            off = FAR[t]
            pair = own[g, t] + sib_r[k, g, t]
            if off in (0, 2, nz - 2):
                own[g, t] = pair
                continue
            rs_s[k, g, off] = pair.astype(BF16)
            if off == 4:
                rs_send(k, g, 4, 2, 0)
                rs_send(k, g, 4, nz - 2, 1)
            elif off == 3:
                rs_send(k, g, 3, 1, 1)
                rs_send(k, g, 3, 1, 0)
            elif off == nz - 3:
                rs_send(k, g, off, nz - 1, 0)
                rs_send(k, g, off, nz - 1, 1)
            else:
                rs_send(k, g, off, off)

    def a2b(k, g):
        for h in (1, 0):
            for off, near, first in ((2, 3, 1), (nz - 2, nz - 3, 0)):
                part = first if h else 1 - first
                sl = slice(part * hr, part * hr + hr)
                rs_wait(k, g, near, part)
                s = own[g, FAR.index(off), sl] + rs_r[k, g, near, sl].astype(F32)
                if not h:
                    rs_wait(k, g, 4, part)
                    s = s + rs_r[k, g, 4, sl].astype(F32)
                rs_s[k, g, off, sl] = s.astype(BF16)
                rs_send(k, g, off, off, part)

    def ag_sem(k, g, rel, half):
        return ag_rs.at[k, g, {(2, 1): 0, (nz - 2, 0): nz}.get((rel, half), rel)]

    def ag_send(k, g, rel, to, half=None):
        there = (rel - to) % nz
        part = pl.ds(0, R) if half is None else pl.ds(half * hr, hr)
        rc(ag.at[k, g, 0, rel, part], ag.at[k, g, 0, there, part], AG, ag_sem(k, g, there, half), zps[to])

    def z_wait(k, g, rel, half=None):
        part = pl.ds(0, R) if half is None else pl.ds(half * hr, hr)
        wait_recv(ag.at[k, g, 0, rel, part], ag_sem(k, g, rel, half))

    def to_sib(k, g, rel, n=1):
        part = pl.ds(rel, n)
        rc(ag.at[k, g, 0, part], ag.at[k, g, 1, part], AS, as_rs.at[k, g, rel], sib)

    def sib_wait(k, g, rel, n=1):
        part = pl.ds(rel, n)
        wait_recv(ag.at[k, g, 1, part], as_rs.at[k, g, rel])

    def a3(k, g, inv_beta, coef):
        s = own[g, FAR.index(0)]
        for off in (1, nz - 1):
            rs_wait(k, g, off)
            s = s + rs_r[k, g, off].astype(F32)
        for off in (2, nz - 2):
            rs_wait(k, g, off, 0)
            rs_wait(k, g, off, 1)
            s = s + rs_r[k, g, off].astype(F32)
        q = s * inv_beta
        if k:
            q = q - coef * q_prev[g]
        q_prev[g] = q
        ag[k, g, 0, 0] = q.astype(BF16)
        for to, h in ((nz - 2, 0), (2, 1), (nz - 2, 1), (2, 0)):
            ag_send(k, g, 0, to, h)
        for to in (1, nz - 1):
            ag_send(k, g, 0, to)
        to_sib(k, g, 0)

    def a4a(k, g):
        z_wait(k, g, 2, 0)
        ag_send(k, g, 2, nz - 2, 0)
        ag_send(k, g, 2, nz - 1, 0)
        z_wait(k, g, nz - 2, 1)
        ag_send(k, g, nz - 2, 2, 1)
        ag_send(k, g, nz - 2, 1, 1)
        z_wait(k, g, 2, 1)
        ag_send(k, g, 2, nz - 1, 1)
        z_wait(k, g, nz - 2, 0)
        ag_send(k, g, nz - 2, 1, 0)
        z_wait(k, g, 1)
        to_sib(k, g, 1, 2)
        z_wait(k, g, nz - 1)
        to_sib(k, g, nz - 2, 2)

    def a4b(k, g):
        for rel in (3, nz - 3, 4):
            z_wait(k, g, rel)
            to_sib(k, g, rel)

    def f1(k, g, rel, poss=(0, 1)):
        vs = [ag[k, g, pos, rel] for pos in poss]
        v = jnp.concatenate(vs, axis=0)
        w = jnp.concatenate([h for u in vs for h in (-u[vr:], u[:vr])], axis=0)
        res = lax.dot_general(v, g_v[:rows, lanes[rel]], NT, preferred_element_type=F32)
        res = res + lax.dot_general(w, g_v[rows:, lanes[rel]], NT, preferred_element_type=F32)
        sl = slice(poss[0] * R, (poss[-1] + 1) * R)
        if rel == 0:
            acc[g, sl] = res
        else:
            acc[g, sl] += res

    def q_norms(k, g, rel):
        for pos in range(2):
            nsq[g, pos, chunks[rel]] = tile_of_squares(ag[k, g, pos, rel].astype(F32))

    YP = [(pos, slice(pos * R + n * hr, pos * R + n * hr + hr), 2 * n + pos) for pos in range(2) for n in range(2)]

    def y_send(k, g, step, poss=(0, 1)):
        for pos, sl, i in YP:
            if pos not in poss:
                continue
            if step:
                wait_recv(y_r.at[k, g, 0, sl], y_rs.at[k, g, 0, i])
                acc[g, sl] = acc[g, sl] + y_r[k, g, 0, sl].astype(F32)
            y_s[k, g, step, sl] = acc[g, sl].astype(BF16)
            dev = ynb[(pos + step) % 2]
            rc(y_s.at[k, g, step, sl], y_r.at[k, g, step, sl], Y, y_rs.at[k, g, step, i], dev)

    def f2(k, g, inv_alpha, coef):
        for pos, sl, i in YP:
            wait_recv(y_r.at[k, g, 1, sl], y_rs.at[k, g, 1, i])
            total = acc[g, sl] + y_r[k, g, 1, sl].astype(F32)
            rs = slice(sl.start - pos * R, sl.stop - pos * R)
            p_st[g, pos, rs] = total * inv_alpha - coef * p_st[g, pos, rs]

    def out_copy(o, rel):
        dst = (x_out, w1_out, q2_out)[o].at[:, pl.ds(pl.multiple_of(chunks[rel] * CH, CH), CH)]
        return pltpu.make_async_copy(out_st.at[o, rel], dst, out_sem.at[o])

    def out_chunk(o, rel, weights):
        for g in G:
            for pos in range(2):
                h = core if pos == 0 else 1 - core
                base = pl.multiple_of(h * half + g * vr, vr)
                if weights is None:
                    val = ag[ITERS, g, pos, rel]
                else:
                    val = sum(c * ag[j, g, pos, rel].astype(F32) for j, c in enumerate(weights)).astype(BF16)
                for c in range(2):
                    out_buf[o, rel, c, pl.ds(base, vr), :] = val[c * vr : (c + 1) * vr]
        for c in range(2):
            out_st[o, rel, c] = out_buf[o, rel, c].T
        out_copy(o, rel).start()

    recur = []

    def advance(beta, alpha=None):
        phibar, rhobar = recur_state[0]
        rho = jnp.sqrt(rhobar * rhobar + beta * beta)
        cosine, sine = rhobar / rho, beta / rho
        if alpha is None:
            return cosine * phibar / rho
        recur_state[0] = (sine * phibar, -cosine * alpha)
        recur.append((cosine * phibar / rho, sine * alpha / rho))

    recur_state = [None]

    data_copy.wait()
    for c in range(2):
        d_t[c] = data_ref[c].T
    for g in G:
        for pos in range(2):
            h = core if pos == 0 else 1 - core
            base = pl.multiple_of(h * half + g * vr, vr)
            for c in range(2):
                p_st[g, pos, c * vr : (c + 1) * vr, :] = d_t[c, pl.ds(base, vr), :]
    build(0, 0)

    alphas, betas = [], []
    for k in range(PH):
        last = k == ITERS
        for g in G:
            if k:
                f2(k - 1, g, inv_alpha, alphas[-1] / betas[-1])
            if k or g:
                build(k, g)
            if k == 0:
                for pos in (1, 0):
                    for batch in range(5):
                        a1(k, g, batch, pos)
                if g == 0:
                    pl.semaphore_wait(barrier, len(peers))
                for batch in range(5):
                    sib_send(k, g, batch)
            else:
                for batch in (0, 1, 2):
                    a1(k, g, batch, 1)
                    sib_send(k, g, batch)
                for batch in (0, 1, 2):
                    a1(k, g, batch, 0)
            if g == GROUPS - 1:
                sp1_send(k)
            for batch in (0, 1, 2):
                a2(k, g, batch)
        for g in G:
            if k:
                for batch in (3, 4):
                    a1(k, g, batch, 1)
                    sib_send(k, g, batch)
                for batch in (3, 4):
                    a1(k, g, batch, 0)
            a2(k, g, 3)
            a2(k, g, 4)
        if last:
            w_1 = (-recur[0][1] / alphas[0], 1.0 / alphas[1])
            for rel in range(nz):
                out_chunk(1, rel, w_1)
        sp1_wait_sp2_send(k)
        for g in G:
            a2b(k, g)
        betas.append(sp2_wait(k))
        inv_beta = 1.0 / betas[-1]
        coef = betas[-1] / alphas[-1] if k else None
        for g in G:
            a3(k, g, inv_beta, coef)
        if last:
            last_norm_send(k)
            step_2 = advance(betas[-1])
            x_w = ((recur[0][0] - step_2 * recur[0][1]) / alphas[0], step_2 / alphas[1])
            for rel in range(nz):
                out_chunk(0, rel, x_w)
            for g in G:
                a4a(k, g)
            last_norm_mid(k)
            for g in G:
                for rel, n in ((0, 1), (1, 2), (nz - 2, 2)):
                    sib_wait(k, g, rel, n)
            for rel in (0, 1, 2, nz - 2, nz - 1):
                out_chunk(2, rel, None)
            for g in G:
                a4b(k, g)
            for rel in (3, nz - 3, 4):
                for g in G:
                    sib_wait(k, g, rel)
                out_chunk(2, rel, None)
            alphas.append(last_norm_wait())
            drain(k)
            advance(betas[-1], alphas[-1])
            break
        for g in G:
            sib_wait(k, g, 0)
            f1(k, g, 0)
        for g in G:
            a4a(k, g)
        for g in G:
            sib_wait(k, g, 1, 2)
            f1(k, g, 1)
            f1(k, g, 2)
            sib_wait(k, g, nz - 2, 2)
            f1(k, g, nz - 2)
            f1(k, g, nz - 1)
        for g in G:
            for rel in (0, 1, 2, nz - 2, nz - 1):
                q_norms(k, g, rel)
        for g in G:
            for rel in (3, nz - 3, 4):
                z_wait(k, g, rel)
                to_sib(k, g, rel)
                f1(k, g, rel, (0,))
            y_send(k, g, 0, (0,))
        for g in G:
            for rel in (3, nz - 3, 4):
                sib_wait(k, g, rel)
                f1(k, g, rel, (1,))
            y_send(k, g, 0, (1,))
        for g in G:
            for rel in (3, nz - 3, 4):
                q_norms(k, g, rel)
        sq_send(k)
        for g in G:
            y_send(k, g, 1)
        drain(k)
        alphas.append(jnp.sqrt(total_of(sq_tile(k))))
        inv_alpha = 1.0 / alphas[-1]
        if k == 0:
            recur_state[0] = (betas[0], alphas[0])
        else:
            advance(betas[-1], alphas[-1])

    factor = math.sqrt(2.0 * nx * cols * ny * width)
    coef_ref[0] = jnp.broadcast_to(factor / alphas[-1], (8, 128))
    coef_ref[1] = jnp.broadcast_to(-factor * recur[-1][1], (8, 128))
    for o in range(3):
        pltpu.make_async_copy(out_st.at[o], out_st.at[o], out_sem.at[o]).wait()


def finish_kernel(x_ref, w1_ref, q2_ref, coef_ref, x_out, w_out):
    for c in range(2):
        x_out[c, 0] = x_ref[c].astype(F32)
        w_out[c, 0] = q2_ref[c].astype(F32) * coef_ref[0, 0:1, 0:1] + w1_ref[c].astype(F32) * coef_ref[1, 0:1, 0:1]


def on_device(nx, ny, nz, kernel, data):
    rows, cols, width = kernel.shape[2], kernel.shape[3], data.shape[3]
    dims = (nx, ny, nz, rows, cols, width)
    R = width // GROUPS
    G = GROUPS
    sem = pltpu.SemaphoreType.DMA
    vm = pltpu.VMEM
    part = jax.ShapeDtypeStruct((2, cols, width), BF16)
    hbm = pl.BlockSpec(memory_space=pl.ANY)
    x_2, w_1, q_2, coefs = pl.pallas_call(
        functools.partial(lsqr_kernel, dims),
        name="lsqr",
        out_shape=(
            part,
            part,
            part,
            jax.ShapeDtypeStruct((2, 8, 128), F32),
        ),
        in_specs=[hbm, hbm],
        out_specs=(hbm, hbm, hbm, pl.BlockSpec(memory_space=pltpu.VMEM)),
        scratch_shapes=[
            vm((2 * rows, cols), BF16),
            vm((2, rows, width), F32),
            vm((2, width, rows), F32),
            vm((G, 2, R, rows), F32),
            vm((G, 2, 2 * R, 2 * rows), BF16),
            vm((G, nz, R, CH), F32),
            vm((G, R, CH), F32),
            vm((G, 2 * R, rows), F32),
            vm((PH, G, nz, R, CH), F32),
            vm((PH, G, nz, R, CH), F32),
            vm((PH, G, nz, R, CH), BF16),
            vm((PH, G, nz, R, CH), BF16),
            vm((PH, G, 2, nz, R, CH), BF16),
            vm((ITERS, G, 2, 2 * R, rows), BF16),
            vm((ITERS, G, 2, 2 * R, rows), BF16),
            vm((G, 2, nz, 8, 128), F32),
            vm((PH, nx * ny, 8, 128), F32),
            vm((PH, 2 * nx, 8, 128), F32),
            vm((PH, nz, 8, 128), F32),
            vm((2 * nz, 8, 128), F32),
            vm((3, nz, 2, width, CH), BF16),
            vm((3, nz, 2, CH, width), BF16),
            sem((nz + 1,)),
            sem((3,)),
            sem((9,)),
            sem((3 * PH + 1,)),
            sem((PH, G, 5)),
            sem((PH, G, 2, nz)),
            sem((PH, G, nz + 1)),
            sem((PH, G, nz)),
            sem((ITERS, G, 2, 4)),
        ],
        compiler_params=pltpu.CompilerParams(collective_id=0, has_side_effects=True, vmem_limit_bytes=56 << 20),
    )(kernel.reshape(2 * rows, cols), data[:, 0])
    out = jax.ShapeDtypeStruct((2, 1, cols, width), F32)
    blk = pl.BlockSpec((2, cols // 2, width), lambda i: (0, i, 0))
    out_blk = pl.BlockSpec((2, 1, cols // 2, width), lambda i: (0, 0, i, 0))
    return pl.pallas_call(
        finish_kernel,
        name="finish",
        grid=(2,),
        out_shape=(out, out),
        in_specs=[blk, blk, blk, pl.BlockSpec((2, 8, 128), lambda i: (0, 0, 0))],
        out_specs=(out_blk, out_blk),
        compiler_params=pltpu.CompilerParams(vmem_limit_bytes=60 << 20),
    )(x_2, w_1, q_2, coefs)


def solution(mesh):
    nx, ny, nz = mesh.shape["freq"], mesh.shape["src"], mesh.shape["rx"] // 2
    return jax.shard_map(
        functools.partial(on_device, nx, ny, nz),
        mesh=mesh,
        in_specs=(P(None, "freq", "rx", "src"), P(None, "freq", "rx", None)),
        out_specs=(P(None, "freq", "src", None), P(None, "freq", "src", None)),
        check_vma=False,
    )
```
